128 devices in a mesh: gx: 8 (over z_hi, y), gy: 16 (over z_lo, x, core).
Axes of the slice: x: 4, y: 4, z: 4 (z_hi: 2, z_lo: 2; z = z_hi * 2 + z_lo), core: 2. Of those that a mesh axis runs over, the one named last changes fastest.
Arguments:
- wind_east: float32 [64, 256, 2048], P(None, 'gx', 'gy'), may hold values from -6 to 6
- wind_north: float32 [64, 256, 2048], P(None, 'gx', 'gy'), may hold values from -6 to 6
- pressure: float32 [64, 256, 2048], P(None, 'gx', 'gy'), may hold values from -6 to 6
- stiffness: float32 [256, 2048], P('gx', 'gy'), may hold values from 8 to 64
- parent_east: float32 [3, 64, 3, 2048], P(None, None, None, 'gy'), may hold values from -6 to 6
- parent_north: float32 [3, 64, 256, 3], P(None, None, 'gx'), may hold values from -6 to 6
- parent_corner: float32 [3, 64, 3, 3], replicated, may hold values from -6 to 6
- offsets: int32 [2], replicated, may hold values from 0 to 3, as said below
Outputs:
- moved_east: float32 [64, 256, 2048], P(None, 'gx', 'gy')
- moved_north: float32 [64, 256, 2048], P(None, 'gx', 'gy')
- moved_pressure: float32 [64, 256, 2048], P(None, 'gx', 'gy')
The draws below stay inside these ranges and needn't reach their ends.
Inputs may be any that keep to these rules, and one draw needn't show every extreme that they name: At least one of the two offsets is 3.
All inputs are finite; a program needn't handle non-finite values.
Results may differ from the reference program's by a relative error of at most 0.00012.
Values sent between devices are 32-bit elements; how exact they have to be, the bound alone decides.
No kernel may reach another device: no remote copies, remote signals or barrier semaphores. Data moves between devices by JAX's collectives and lax.ppermute only.
A program may use at most 128 MiB of HBM per device.

```python
import math
import jax
import jax.numpy as jnp
from jax import lax

L = 64
STEPS = 2
NX = 256
NY = 2048


def draw_offsets(key, part):
    key = jax.random.fold_in(key, 23)
    pick = jax.random.randint(key, (), 0, 7).astype(jnp.int32)
    three = jnp.full((), 3, jnp.int32)
    east_value = jnp.where(pick < 4, three, pick - 4)
    north_value = jnp.where(pick < 4, pick, three)
    return jnp.stack([east_value, north_value]).astype(jnp.int32)


def block_scale(rng, extent, split, smallest, high):
    def one(axis_at, parts):
        heights = jax.random.uniform(jax.random.fold_in(jax.random.fold_in(rng, 6), axis_at), (parts,), jnp.float32, smallest / len(split), high / len(split))
        return jnp.repeat(jnp.exp(heights), extent[axis_at] // parts).reshape((-1,) + (1,) * (len(extent) - axis_at - 1))

    level = one(*split[0])
    for cut in split[1:]:
        level = level * one(*cut)
    return level


def scatter_about(rng, dims, scale, most, split=(), kind=jnp.bfloat16):
    values = scale * jax.random.normal(rng, dims, jnp.float32)
    if split:
        values = values * block_scale(rng, dims, split, -0.22, 0.18)
    return jnp.clip(values, -most, most).astype(kind)


def setup_inputs(seed: int = 0) -> dict:
    seeds = jax.random.split(jax.random.key(seed), 9)
    wind_east = scatter_about(seeds[0], (L, NX, NY), 1.0, 6.0, ((1, 8), (2, 16)), jnp.float32)
    wind_north = scatter_about(seeds[1], (L, NX, NY), 1.0, 6.0, ((1, 8), (2, 16)), jnp.float32)
    pressure = scatter_about(seeds[2], (L, NX, NY), 1.0, 6.0, ((1, 8), (2, 16)), jnp.float32)
    stiffness = jnp.clip(jnp.exp(math.log(64.0) - 2.0794415 * jax.random.uniform(seeds[3], (NX, NY), jnp.float32) ** block_scale(seeds[3], (NX, NY), ((0, 8), (1, 16)), -0.2, 0.2)), 8.0, 64.0)
    parent_east = scatter_about(seeds[4], (3, L, 3, NY), 1.0, 6.0, ((3, 16),), jnp.float32)
    parent_north = scatter_about(seeds[5], (3, L, NX, 3), 1.0, 6.0, ((2, 8),), jnp.float32)
    parent_corner = scatter_about(seeds[6], (3, L, 3, 3), 1.0, 6.0, (), jnp.float32)
    offsets = draw_offsets(jax.random.fold_in(seeds[8], 71), 0)
    return {"wind_east": wind_east, "wind_north": wind_north, "pressure": pressure, "stiffness": stiffness, "parent_east": parent_east, "parent_north": parent_north, "parent_corner": parent_corner, "offsets": offsets}


courant = 0.6


def centred(field, axis):
    length = field.shape[axis] - 6

    def part(offset):
        return lax.slice_in_dim(field, 3 + offset, 3 + offset + length, axis=axis)

    return 0.75 * (part(1) - part(-1)) - 0.15 * (part(2) - part(-2)) + (part(3) - part(-3)) / 60.0


def column_solve(rhs, stiffness):
    levels = rhs.shape[0]
    level_index = jnp.arange(levels)
    has_below = (level_index > 0).astype(rhs.dtype)
    has_above = (level_index < levels - 1).astype(rhs.dtype)

    def forward(carry, inputs):
        upper_prev, value_prev = carry
        source, below, above_flag = inputs
        divisor = 1.0 + stiffness * (below + above_flag) + stiffness * below * upper_prev
        upper_next = -stiffness * above_flag / divisor
        value_next = (source + stiffness * below * value_prev) / divisor
        return (upper_next, value_next), (upper_next, value_next)

    start = (jnp.zeros_like(rhs[0]), jnp.zeros_like(rhs[0]))
    ignored, (uppers, values) = lax.scan(forward, start, (rhs, has_below, has_above))

    def backward(later, inputs):
        upper, value = inputs
        current = value - upper * later
        return current, current

    ignored_last, solved = lax.scan(backward, jnp.zeros_like(rhs[0]), (uppers, values), reverse=True)
    return solved


def reference(wind_east, wind_north, pressure, stiffness, parent_east, parent_north, parent_corner, offsets):
    for substep in range(STEPS):
        padded = jnp.pad(pressure, ((0, 0), (3, 3), (3, 3)))
        wind_east = wind_east - courant * centred(padded[:, :, 3:-3], 1)
        wind_north = wind_north - courant * centred(padded[:, 3:-3, :], 2)
        east_pad = jnp.pad(wind_east, ((0, 0), (3, 3), (0, 0)))
        north_pad = jnp.pad(wind_north, ((0, 0), (0, 0), (3, 3)))
        rhs = pressure - courant * (centred(east_pad, 1) + centred(north_pad, 2))
        pressure = column_solve(rhs, stiffness)
    fields = jnp.stack((wind_east, wind_north, pressure))
    upper_band = jnp.concatenate([fields, parent_north], axis=3)
    lower_band = jnp.concatenate([parent_east, parent_corner], axis=3)
    extended = jnp.concatenate([upper_band, lower_band], axis=2)
    anchor = jnp.zeros((), jnp.int32)
    moved = lax.dynamic_slice(extended, (anchor, anchor, offsets[0].astype(jnp.int32), offsets[1].astype(jnp.int32)), fields.shape)
    return moved[0], moved[1], moved[2]
```

```python
import functools

import jax
import jax.numpy as jnp
import numpy as np
from jax import lax
from jax.experimental import pallas as pl
from jax.experimental.pallas import tpu as pltpu
from jax.sharding import PartitionSpec as P

F32 = jnp.float32
BF16 = jnp.bfloat16

C1, C2, C3 = 0.45, 0.09, 0.01
CY = 0.01


def band():
    mat = np.zeros((256, 256), np.float32)
    for j in range(256):
        for k, w in ((1, 45.0), (2, -9.0), (3, 1.0)):
            mat[(j + k) % 256, j] = w
            mat[(j - k) % 256, j] = -w
    return mat


def swaps(count):
    inner = [(i, i ^ 1) for i in range(count)]
    outer = [(i, min(max(((i + 1) ^ 1) - 1, 0), count - 1)) for i in range(count)]
    return inner, outer


def lane_index():
    return lax.broadcasted_iota(jnp.int32, (1, 128), 1)


def roll_lanes(value, shift):
    return pltpu.roll(value, shift % 128, 1)


def dy(ext, mat):
    hi = ext.astype(BF16)
    lo = (ext - hi.astype(F32)).astype(BF16)
    return jnp.dot(hi, mat, preferred_element_type=F32) + jnp.dot(
        lo, mat, preferred_element_type=F32
    )


def pack(rows, width, step, lanes):
    out = None
    for m, row in enumerate(rows):
        moved = roll_lanes(row, m * step + width)
        out = moved if out is None else jnp.where(lanes >= m * step, moved, out)
    return out


def x_edges_kernel(meta, p, u, first, second):
    def write(ref, low):
        for l in range(64):
            a = 0 if low else 26
            ref[6 * l : 6 * l + 6, :] = p[l, a : a + 6, :]
            a = 0 if low else 29
            ref[384 + 3 * l : 387 + 3 * l, :] = u[l, a : a + 3, :]

    even = meta[0] % 2 == 0

    @pl.when(even)
    def _():
        write(first, False)
        write(second, True)

    @pl.when(jnp.logical_not(even))
    def _():
        write(first, True)
        write(second, False)


def y_edges_kernel(p, v, out):
    lanes = lane_index()
    for b in range(8):
        out[b] = pack([p[8 * b + m] for m in range(8)], 6, 16, lanes)
    for b in range(4):
        out[8 + b] = pack([v[16 * b + m] for m in range(16)], 3, 8, lanes)


def coefficients_kernel(s_ref, inv_ref):
    s = s_ref[...]
    prev = None
    for l in range(64):
        if l == 0:
            div = 1.0 + s
        elif l < 63:
            div = 1.0 + 2.0 * s - s * (s * prev)
        else:
            div = 1.0 + s - s * (s * prev)
        prev = 1.0 / div
        inv_ref[l] = prev


def put_halo(buf, first, second, meta, start, rows, width):
    even = meta[0] % 2 == 0
    west_in = meta[0] > 0
    east_in = meta[0] < meta[2] - 1

    def write(ref, west):
        ok = west_in if west else east_in
        for l in range(64):
            part = ref[start + rows * l : start + rows * (l + 1), :]
            part = jnp.where(ok, part, 0.0)
            if west:
                buf[l, 8 - width : 8, :] = part
            else:
                buf[l, 40 : 40 + width, :] = part

    @pl.when(even)
    def _():
        write(first, False)
        write(second, True)

    @pl.when(jnp.logical_not(even))
    def _():
        write(first, True)
        write(second, False)


def row_mask(meta):
    rows = lax.broadcasted_iota(jnp.int32, (40, 128), 0)
    west = jnp.where(meta[0] > 0, 1.0, 0.0)
    east = jnp.where(meta[0] < meta[2] - 1, 1.0, 0.0)
    return jnp.where(rows < 3, west, jnp.where(rows >= 35, east, 1.0))


def substep(meta, p, u_of, v_of, vh_of, s_ref, inv, mat, y1, y2, pp, u_out, v_out, vh_out, w_buf, p_out):
    lanes = lane_index()
    even_y = meta[1] % 2 == 0
    in_s = meta[1] > 0
    in_n = meta[1] < meta[3] - 1
    lane_ok = jnp.where(lanes < 64, jnp.where(in_n, 1.0, 0.0), jnp.where(in_s, 1.0, 0.0))
    rmask = row_mask(meta)
    s = s_ref[...]

    def sides(b, low):
        a, c = y1[b], y2[b]
        north = jnp.where(in_n, jnp.where(even_y, a, c), 0.0)
        south = jnp.where(in_s, jnp.where(even_y, c, a), 0.0)
        return jnp.where(low, south, north)

    w = jnp.zeros((32, 128), F32)
    for b in range(8):
        blk = sides(b, lanes % 16 < 6)
        halo = jnp.concatenate([roll_lanes(blk, -(16 * m + 6)) for m in range(8)], axis=0)
        own = p[8 * b : 8 * b + 8].reshape(256, 128)
        d = dy(jnp.concatenate([own, halo], axis=1), mat[...])
        v1 = v_of(b) - CY * d[:, :128]
        vh = (vh_of(b, sides) - CY * d[:, 128:]) * lane_ok
        v_out[8 * b : 8 * b + 8] = v1.reshape(8, 32, 128)
        vh_out[8 * b : 8 * b + 8] = vh.reshape(8, 32, 128)
        d2 = dy(jnp.concatenate([v1, vh], axis=1), mat[:, :128])
        rest = own - CY * d2
        for m in range(8):
            l = 8 * b + m
            pp[l, 8:40, :] = own[32 * m : 32 * m + 32]
            d1 = pp[l, 6:46, :] - pp[l, 4:44, :]
            d2x = pp[l, 7:47, :] - pp[l, 3:43, :]
            d3 = pp[l, 8:48, :] - pp[l, 2:42, :]
            u1 = (u_of(l) - (C1 * d1 - C2 * d2x + C3 * d3)) * rmask
            u_out[l, 5:45, :] = u1
            e1 = u_out[l, 9:41, :] - u_out[l, 7:39, :]
            e2 = u_out[l, 10:42, :] - u_out[l, 6:38, :]
            e3 = u_out[l, 11:43, :] - u_out[l, 5:37, :]
            rhs = rest[32 * m : 32 * m + 32] - (C1 * e1 - C2 * e2 + C3 * e3)
            w = (rhs + s * w) * inv[l]
            w_buf[l] = w
    q = jnp.zeros((32, 128), F32)
    for l in range(63, -1, -1):
        q = w_buf[l] + (s * inv[l]) * q
        p_out[l] = q


def step1_kernel(meta, p, u, v, s, inv, mat, x1, x2, y1, y2, p_out, u_out, v_out, vh_out, first, second, y_out, pp, up, w_buf):
    lanes = lane_index()
    put_halo(pp, x1, x2, meta, 0, 6, 6)
    put_halo(up, x1, x2, meta, 384, 3, 3)

    def u_of(l):
        up[l, 8:40, :] = u[l]
        return up[l, 5:45, :]

    def v_of(b):
        return v[8 * b : 8 * b + 8].reshape(256, 128)

    def vh_of(b, sides):
        blk = sides(8 + b // 2, lanes % 8 < 3)
        at = 64 * (b % 2) + 3
        return jnp.concatenate([roll_lanes(blk, -(at + 8 * m)) for m in range(8)], axis=0)

    substep(meta, p, u_of, v_of, vh_of, s, inv, mat, y1, y2, pp, u_out, v_out, vh_out, w_buf, p_out)

    def write(ref, low):
        a = 0 if low else 26
        for l in range(64):
            ref[6 * l : 6 * l + 6, :] = p_out[l, a : a + 6, :]

    even = meta[0] % 2 == 0

    @pl.when(even)
    def _():
        write(first, False)
        write(second, True)

    @pl.when(jnp.logical_not(even))
    def _():
        write(first, True)
        write(second, False)

    for b in range(8):
        y_out[b] = pack([p_out[8 * b + m] for m in range(8)], 6, 16, lanes)


def step2_kernel(meta, p, u, v, vh, s, inv, mat, x1, x2, y1, y2, pe, p_out, u_out, v_out, e_out, n_out, pp, vh_buf, w_buf):
    lanes = lane_index()
    put_halo(pp, x1, x2, meta, 0, 6, 6)

    def u_of(l):
        return u[l, 5:45, :]

    def v_of(b):
        return v[8 * b : 8 * b + 8].reshape(256, 128)

    def vh_of(b, sides):
        return vh[8 * b : 8 * b + 8].reshape(256, 128)

    substep(meta, p, u_of, v_of, vh_of, s, inv, mat, y1, y2, pp, u_out, v_out, vh_buf, w_buf, p_out)
    for l in range(64):
        e_out[6 * l : 6 * l + 3, :] = p_out[l, 0:3, :]
        e_out[6 * l + 3 : 6 * l + 6, :] = v_out[l, 0:3, :]
    for b in range(8):
        out = None
        for m in range(8):
            l = 8 * b + m
            for f, val in enumerate((u_out[l, 8:40, :], v_out[l], p_out[l])):
                at = 16 * m + 3 * f
                moved = roll_lanes(val, at)
                out = moved if out is None else jnp.where(lanes >= at, moved, out)
        n_out[b, 0:32, :] = out
        n_out[b, 32:40, :] = pe[b]


def move_kernel(meta, u, v, p, e, pe, north, corner, ou, ov, op, ext, ns):
    lanes = lane_index()
    o0, o1 = meta[4], meta[5]
    last_east = meta[0] == meta[2] - 1
    ns[0:32, :] = north[0, 0:32, :]
    ns[32:40, :] = jnp.where(last_east, north[0, 32:40, :], corner[0])
    nrow = ns[pl.ds(o0, 32), :]
    own_lane = lanes < 128 - o1
    shift = lax.rem(128 - o1, 128)
    for m in range(8):
        for f, out in enumerate((ou, ov, op)):
            buf = ext.at[(3 * m + f) % 6]
            if f == 0:
                buf[0:32, :] = u[m, 8:40, :]
                buf[32:40, :] = u[m, 40:48, :]
            else:
                src = v if f == 1 else p
                at = 6 * m + (3 if f == 1 else 0)
                buf[0:32, :] = src[m]
                buf[32:35, :] = e[at : at + 3, :]
            buf[32:40, :] = jnp.where(last_east, pe[f, m], buf[32:40, :])
            body = buf[pl.ds(o0, 32), :]
            back = lax.rem(256 - (16 * m + 3 * f) - o1, 128)
            out[m] = jnp.where(own_lane, pltpu.roll(body, shift, 1), pltpu.roll(nrow, back, 1))


VMEM = pl.BlockSpec(memory_space=pltpu.VMEM)
SMEM = pl.BlockSpec(memory_space=pltpu.SMEM)


def call(body, out_shape, args, scratch=(), name=None, flops=0):
    size = sum(int(np.prod(a.shape)) * a.dtype.itemsize for a in args)
    size += sum(int(np.prod(o.shape)) * o.dtype.itemsize for o in jax.tree.leaves(out_shape))
    specs = [SMEM if a.ndim == 1 else VMEM for a in args]
    return pl.pallas_call(
        body,
        out_shape=out_shape,
        in_specs=specs,
        out_specs=jax.tree.map(lambda _: VMEM, out_shape),
        scratch_shapes=list(scratch),
        name=name,
        cost_estimate=pl.CostEstimate(flops=flops, bytes_accessed=size, transcendentals=0),
        compiler_params=pltpu.CompilerParams(vmem_limit_bytes=40 << 20),
    )(*args)


def on_device(wind_east, wind_north, pressure, stiffness, parent_east, parent_north, parent_corner, offsets):
    def sds(*shape):
        return jax.ShapeDtypeStruct(shape, F32)

    nx, ny = lax.axis_size("gx"), lax.axis_size("gy")
    gx, gy = lax.axis_index("gx"), lax.axis_index("gy")
    meta = jnp.stack(
        [gx, gy, jnp.int32(nx), jnp.int32(ny), offsets[0], offsets[1]]
    ).astype(jnp.int32)
    mat = jnp.asarray(band(), BF16)
    x_in, x_out = swaps(nx)
    y_in, y_out = swaps(ny)
    scratch_field = pltpu.VMEM((64, 32, 128), F32)
    scratch_padded = pltpu.VMEM((64, 48, 128), F32)

    first, second = call(
        x_edges_kernel, (sds(576, 128), sds(576, 128)), (meta, pressure, wind_east), name="x_edges"
    )
    x2 = lax.ppermute(second, "gx", x_out)
    x1 = lax.ppermute(first, "gx", x_in)
    strip = call(y_edges_kernel, sds(12, 32, 128), (pressure, wind_north), name="y_edges")
    y1 = lax.ppermute(strip, "gy", y_in)
    y2 = lax.ppermute(strip, "gy", y_out)
    inv = call(coefficients_kernel, sds(64, 32, 128), (stiffness,), name="coefficients")

    def strips(value):
        rows = value.shape[2]
        value = value.reshape(3, 8, 8, rows, 3).transpose(1, 3, 2, 0, 4).reshape(8, rows, 8, 9)
        return jnp.pad(value, ((0, 0), (0, 0), (0, 0), (0, 7))).reshape(8, rows, 128)

    pe_strip = jnp.pad(strips(parent_east[:, :, :, :3]), ((0, 0), (0, 5), (0, 0)))
    pn_strip = jnp.concatenate([strips(parent_north), strips(parent_corner)], axis=1)
    pn_strip = jnp.pad(pn_strip, ((0, 0), (0, 5), (0, 0)))
    pe_rows = jnp.pad(parent_east, ((0, 0), (0, 0), (0, 5), (0, 0)))

    p1, u1, v1, vh1, first, second, strip = call(
        step1_kernel,
        (sds(64, 32, 128), sds(64, 48, 128), sds(64, 32, 128), sds(64, 32, 128), sds(384, 128), sds(384, 128), sds(8, 32, 128)),
        (meta, pressure, wind_east, wind_north, stiffness, inv, mat, x1, x2, y1, y2),
        (scratch_padded, scratch_padded, scratch_field),
        name="step1",
    )
    x2 = lax.ppermute(second, "gx", x_out)
    x1 = lax.ppermute(first, "gx", x_in)
    y1 = lax.ppermute(strip, "gy", y_in)
    y2 = lax.ppermute(strip, "gy", y_out)
    p2, u2, v2, east, north = call(
        step2_kernel,
        (sds(64, 32, 128), sds(64, 48, 128), sds(64, 32, 128), sds(384, 128), sds(8, 40, 128)),
        (meta, p1, u1, v1, vh1, stiffness, inv, mat, x1, x2, y1, y2, pe_strip),
        (scratch_padded, scratch_field, scratch_field),
        name="step2",
    )
    down_x = [(i, (i - 1) % nx) for i in range(nx)]
    down_y = [(j, (j - 1) % ny) for j in range(ny)]
    from_north = lax.ppermute(north, "gy", down_y)
    from_east = lax.ppermute(east, "gx", down_x)
    north = jnp.where(gy == ny - 1, pn_strip, from_north)
    corner = lax.ppermute(north[:, :8, :], "gx", down_x)

    def block(*shape):
        return pl.BlockSpec(shape, lambda b: (b,) + (0,) * (len(shape) - 1))

    field = block(8, 32, 128)
    return pl.pallas_call(
        move_kernel,
        grid=(8,),
        out_shape=(sds(64, 32, 128),) * 3,
        in_specs=[
            SMEM,
            block(8, 48, 128),
            field,
            field,
            block(48, 128),
            pl.BlockSpec((3, 8, 8, 128), lambda b: (0, b, 0, 0)),
            block(1, 40, 128),
            block(1, 8, 128),
        ],
        out_specs=(field,) * 3,
        scratch_shapes=[pltpu.VMEM((6, 40, 128), F32), pltpu.VMEM((40, 128), F32)],
        name="move",
        compiler_params=pltpu.CompilerParams(vmem_limit_bytes=24 << 20),
    )(meta, u2, v2, p2, from_east, pe_rows, north, corner)


def solution(mesh):
    in_specs = (
        P(None, "gx", "gy"),
        P(None, "gx", "gy"),
        P(None, "gx", "gy"),
        P("gx", "gy"),
        P(None, None, None, "gy"),
        P(None, None, "gx", None),
        P(),
        P(),
    )
    out_specs = (P(None, "gx", "gy"), P(None, "gx", "gy"), P(None, "gx", "gy"))
    return jax.shard_map(
        on_device, mesh=mesh, in_specs=in_specs, out_specs=out_specs, check_vma=False
    )
```

```python
import functools

import jax
import jax.numpy as jnp
import numpy as np
from jax import lax
from jax.experimental import pallas as pl
from jax.experimental.pallas import tpu as pltpu
from jax.sharding import PartitionSpec as P

F32 = jnp.float32
BF16 = jnp.bfloat16

C1, C2, C3 = 0.45, 0.09, 0.01
CY = 0.01


def band():
    mat = np.zeros((256, 256), np.float32)
    for j in range(256):
        for k, w in ((1, 45.0), (2, -9.0), (3, 1.0)):
            mat[(j + k) % 256, j] = w
            mat[(j - k) % 256, j] = -w
    return mat


def swaps(count):
    inner = [(i, i ^ 1) for i in range(count)]
    outer = [(i, min(max(((i + 1) ^ 1) - 1, 0), count - 1)) for i in range(count)]
    return inner, outer


def lane_index():
    return lax.broadcasted_iota(jnp.int32, (1, 128), 1)


def roll_lanes(value, shift):
    return pltpu.roll(value, shift % 128, 1)


def dy(ext, mat):
    hi = ext.astype(BF16)
    lo = (ext - hi.astype(F32)).astype(BF16)
    return jnp.dot(hi, mat, preferred_element_type=F32) + jnp.dot(
        lo, mat, preferred_element_type=F32
    )


def pack(rows, width, step, lanes):
    out = None
    for m, row in enumerate(rows):
        moved = roll_lanes(row, m * step + width)
        out = moved if out is None else jnp.where(lanes >= m * step, moved, out)
    return out


def write_edges(buffers, east, first, second):
    def write(ref, side):
        at = 0
        for buf, width in buffers[side]:
            a = 0 if side == 0 else 8 - width
            for l in range(64):
                ref[at + width * l : at + width * (l + 1), :] = buf[l, a : a + width, :]
            at += 64 * width

    @pl.when(east)
    def _():
        write(first, 1)
        write(second, 0)

    @pl.when(jnp.logical_not(east))
    def _():
        write(first, 0)
        write(second, 1)


def x_edges_kernel(p, u, first, second, pw, pe, uw, ue, sems):
    copies = []
    for k, (src, buf, at) in enumerate(((p, pw, 0), (u, uw, 0), (p, pe, 24), (u, ue, 24))):
        copies.append(pltpu.make_async_copy(src.at[:, at : at + 8, :], buf, sems.at[k]))
    for copy in copies:
        copy.start()
    for copy in copies:
        copy.wait()
    even = lax.axis_index("gx") % 2 == 0
    write_edges((((pw, 6), (uw, 3)), ((pe, 6), (ue, 3))), even, first, second)


def y_edges_kernel(p, v, out):
    lanes = lane_index()
    for b in range(8):
        out[b] = pack([p[8 * b + m] for m in range(8)], 6, 16, lanes)
    for b in range(4):
        out[8 + b] = pack([v[16 * b + m] for m in range(16)], 3, 8, lanes)


def y_pack_kernel(p, out):
    lanes = lane_index()
    for b in range(8):
        out[b] = pack([p[8 * b + m] for m in range(8)], 6, 16, lanes)


def coefficients_kernel(s_ref, inv_ref, g_ref):
    s = s_ref[...]
    prev = None
    for l in range(64):
        if l == 0:
            div = 1.0 + s
        elif l < 63:
            div = 1.0 + 2.0 * s - s * prev
        else:
            div = 1.0 + s - s * prev
        inv = 1.0 / div
        inv_ref[l] = inv
        prev = s * inv
        g_ref[l] = prev


def difference(at):
    return C1 * (at(1) - at(-1)) - C2 * (at(2) - at(-2)) + C3 * (at(3) - at(-3))


def inner_kernel(first_step, p, u, v, *rest):
    if first_step:
        inv, g, mat, y1, y2, keep1, keep2, keep3, p_out, u_out, v_out, vh_out, rest_out, w_buf = rest
        du = 0
    else:
        vh_in, inv, g, mat, y1, y2, p_out, u_out, v_out, rest_out, w_buf = rest
        du = 8
    lanes = lane_index()
    gy = lax.axis_index("gy")
    even_y = gy % 2 == 0
    in_s = gy > 0
    in_n = gy < lax.axis_size("gy") - 1
    lane_ok = jnp.where(lanes < 64, jnp.where(in_n, 1.0, 0.0), jnp.where(in_s, 1.0, 0.0))

    def sides(b, low):
        a, c = y1[b], y2[b]
        north = jnp.where(in_n, jnp.where(even_y, a, c), 0.0)
        south = jnp.where(in_s, jnp.where(even_y, c, a), 0.0)
        return jnp.where(low, south, north)

    w = jnp.zeros((16, 128), F32)
    for b in range(8):
        blk = sides(b, lanes % 16 < 6)
        halo = jnp.concatenate([roll_lanes(blk, -(16 * m + 6)) for m in range(8)], axis=0)
        if first_step:
            blk = sides(8 + b // 2, lanes % 8 < 3)
            at = 64 * (b % 2) + 3
            vh = jnp.concatenate([roll_lanes(blk, -(at + 8 * m)) for m in range(8)], axis=0)
        else:
            vh = vh_in[8 * b : 8 * b + 8].reshape(256, 128)
        own = p[8 * b : 8 * b + 8].reshape(256, 128)
        d = dy(jnp.concatenate([own, halo], axis=1), mat[...])
        v1 = v[8 * b : 8 * b + 8].reshape(256, 128) - CY * d[:, :128]
        vh = (vh - CY * d[:, 128:]) * lane_ok
        v_out[8 * b : 8 * b + 8] = v1.reshape(8, 32, 128)
        if first_step:
            vh_out[8 * b : 8 * b + 8] = vh.reshape(8, 32, 128)
        d2 = dy(jnp.concatenate([v1, vh], axis=1), mat[:, :128])
        left = own - CY * d2
        for m in range(8):
            l = 8 * b + m
            row = left[32 * m : 32 * m + 32]
            rest_out[l, 0:8, :] = row[0:8]
            rest_out[l, 8:16, :] = row[24:32]
            step = difference(lambda k: p[l, 5 + k : 29 + k, :])
            u_out[l, 13:37, :] = u[l, du + 5 : du + 29, :] - step
            rhs = row[8:24] - difference(lambda k: u_out[l, 16 + k : 32 + k, :])
            w = rhs * inv[l, 8:24, :] + g[l, 8:24, :] * w
            w_buf[l] = w
    q = jnp.zeros((16, 128), F32)
    for l in range(63, -1, -1):
        q = w_buf[l] + g[l, 8:24, :] * q
        p_out[l, 8:24, :] = q


def outer_kernel(first_step, x1, x2, p, u, inv, g, rest, p_in, u_in, *tail):
    if first_step:
        p_out, u_out, first, second, pw, pe, uw, ue, w_buf = tail
    else:
        v, pn, p_out, u_out, east, pw, pe, w_buf = tail
    gx = lax.axis_index("gx")
    even = gx % 2 == 0
    in_w = gx > 0
    in_e = gx < lax.axis_size("gx") - 1

    def fill(ref, west):
        for l in range(64):
            part = jnp.where(in_w if west else in_e, ref[6 * l : 6 * l + 6, :], 0.0)
            if west:
                pw[l, 2:8, :] = part
            else:
                pe[l, 8:14, :] = part
            if first_step:
                part = ref[384 + 3 * l : 387 + 3 * l, :]
                if west:
                    uw[l, 5:8, :] = part
                else:
                    ue[l, 8:11, :] = part

    @pl.when(even)
    def _():
        fill(x1, False)
        fill(x2, True)

    @pl.when(jnp.logical_not(even))
    def _():
        fill(x1, True)
        fill(x2, False)

    rows = lax.broadcasted_iota(jnp.int32, (8, 128), 0)
    ok_w = jnp.where(rows < 3, jnp.where(in_w, 1.0, 0.0), 1.0)
    ok_e = jnp.where(rows >= 3, jnp.where(in_e, 1.0, 0.0), 1.0)
    w = jnp.zeros((16, 128), F32)
    for l in range(64):
        pw[l, 8:16, :] = p[l, 0:8, :]
        pe[l, 0:8, :] = p[l, 24:32, :]
        if first_step:
            uw[l, 8:16, :] = u[l, 0:8, :]
            ue[l, 0:8, :] = u[l, 24:32, :]
            old_w, old_e = uw[l, 5:13, :], ue[l, 5:13, :]
        else:
            old_w, old_e = u[l, 5:13, :], u[l, 37:45, :]
        u_out[l, 5:13, :] = (old_w - difference(lambda k: pw[l, 5 + k : 13 + k, :])) * ok_w
        u_out[l, 37:45, :] = (old_e - difference(lambda k: pe[l, 5 + k : 13 + k, :])) * ok_e
        rhs_w = rest[l, 0:8, :] - difference(lambda k: u_out[l, 8 + k : 16 + k, :])
        rhs_e = rest[l, 8:16, :] - difference(lambda k: u_out[l, 32 + k : 40 + k, :])
        rhs = jnp.concatenate([rhs_w, rhs_e], axis=0)
        il = jnp.concatenate([inv[l, 0:8, :], inv[l, 24:32, :]], axis=0)
        gl = jnp.concatenate([g[l, 0:8, :], g[l, 24:32, :]], axis=0)
        w = rhs * il + gl * w
        w_buf[l] = w
    q = jnp.zeros((16, 128), F32)
    for l in range(63, -1, -1):
        gl = jnp.concatenate([g[l, 0:8, :], g[l, 24:32, :]], axis=0)
        q = w_buf[l] + gl * q
        p_out[l, 0:8, :] = q[0:8]
        p_out[l, 24:32, :] = q[8:16]
        w_buf[l] = q
    if first_step:
        write_edges((((w_buf.at[:, 0:8, :], 6),), ((w_buf.at[:, 8:16, :], 6),)), even, first, second)
    else:
        for l in range(64):
            east[6 * l : 6 * l + 3, :] = w_buf[l, 0:3, :]
            east[6 * l + 3 : 6 * l + 6, :] = v[l, 0:3, :]
        for b in range(8):
            east[384 + 8 * b : 392 + 8 * b, :] = pn[b, 0:8, :]


def north_pack_kernel(u, v, p, pe, out):
    lanes = lane_index()
    for b in range(8):
        strip = None
        for m in range(8):
            l = 8 * b + m
            for f, val in enumerate((u[l, 8:40, :], v[l], p[l])):
                at = 16 * m + 3 * f
                moved = roll_lanes(val, at)
                strip = moved if strip is None else jnp.where(lanes >= at, moved, strip)
        out[b, 0:32, :] = strip
        out[b, 32:40, :] = pe[b]


def turn_kernel(offsets, u, v, p, pe, ru, rv, rp, tail):
    shift = lax.rem(128 - offsets[1], 128)
    last_east = lax.axis_index("gx") == lax.axis_size("gx") - 1
    for l in range(64):
        ru[l] = pltpu.roll(u[l, 8:40, :], shift, 1)
        rv[l] = pltpu.roll(v[l], shift, 1)
        rp[l] = pltpu.roll(p[l], shift, 1)
        tail[0, l] = pltpu.roll(jnp.where(last_east, pe[0, l], u[l, 40:48, :]), shift, 1)
        tail[1, l] = pltpu.roll(pe[1, l], shift, 1)
        tail[2, l] = pltpu.roll(pe[2, l], shift, 1)


def move_kernel(offsets, ru, rv, rp, tail, e, north, ne, pn, ou, ov, op, bu, bv, bp, ext, ns, sems):
    lanes = lane_index()
    o0, o1 = offsets[0], offsets[1]
    last_east = lax.axis_index("gx") == lax.axis_size("gx") - 1
    last_north = lax.axis_index("gy") == lax.axis_size("gy") - 1
    own_lane = lanes < 128 - o1
    shift = lax.rem(128 - o1, 128)
    copies = []
    for b in range(8):
        ns[b, 0:32, :] = jnp.where(last_north, pn[b, 0:32, :], north[b, 0:32, :])
        top = jnp.where(last_east, pn[b, 32:40, :], e[384 + 8 * b : 392 + 8 * b, :])
        low = jnp.where(last_east, north[b, 32:40, :], ne[b])
        ns[b, 32:40, :] = jnp.where(last_north, top, low)
        nrow = ns[b, pl.ds(o0, 32), :]
        for m in range(8):
            l = 8 * b + m
            new = pltpu.roll(e[6 * l : 6 * l + 6, :], shift, 1)
            for f, (src, buf) in enumerate(((ru, bu), (rv, bv), (rp, bp))):
                ext[f, l, 0:8, :] = src[l, 24:32, :]
                ext[f, l, 8:16, :] = tail[f, l]
                if f > 0:
                    part = new[3:6] if f == 1 else new[0:3]
                    ext[f, l, 8:11, :] = jnp.where(last_east, tail[f, l, 0:3, :], part)
                back = lax.rem(256 - (16 * m + 3 * f) - o1, 128)
                strip = pltpu.roll(nrow, back, 1)
                buf[l, 0:24, :] = jnp.where(own_lane, src[l, pl.ds(o0, 24), :], strip[0:24])
                buf[l, 24:32, :] = jnp.where(own_lane, ext[f, l, pl.ds(o0, 8), :], strip[24:32])
        for f, (buf, out) in enumerate(((bu, ou), (bv, ov), (bp, op))):
            part = pl.ds(8 * b, 8)
            copy = pltpu.make_async_copy(buf.at[part], out.at[part], sems.at[8 * f + b])
            copy.start()
            copies.append(copy)
    for copy in copies:
        copy.wait()


VMEM = pl.BlockSpec(memory_space=pltpu.VMEM)
SMEM = pl.BlockSpec(memory_space=pltpu.SMEM)
ANY = pl.BlockSpec(memory_space=pl.ANY)


def sds(*shape):
    return jax.ShapeDtypeStruct(shape, F32)


def buffers(*shapes):
    return [pltpu.VMEM(shape, F32) for shape in shapes]


def call(body, out_shape, args, scratch=(), name=None, specs=None, outs=None, alias=None, us=1.0):
    specs = {} if specs is None else specs
    return pl.pallas_call(
        body,
        out_shape=out_shape,
        in_specs=[specs.get(k, VMEM) for k in range(len(args))],
        out_specs=jax.tree.map(lambda _: outs or VMEM, out_shape),
        scratch_shapes=list(scratch),
        input_output_aliases=alias or {},
        name=name,
        cost_estimate=pl.CostEstimate(flops=0, bytes_accessed=int(us * 3.2e6), transcendentals=0),
        compiler_params=pltpu.CompilerParams(vmem_limit_bytes=16 << 20),
    )(*args)


def on_device(wind_east, wind_north, pressure, stiffness, parent_east, parent_north, parent_corner, offsets):
    nx, ny = lax.axis_size("gx"), lax.axis_size("gy")
    mat = jnp.asarray(band(), BF16)
    x_in, x_out = swaps(nx)
    y_in, y_out = swaps(ny)
    field, padded, outer = sds(64, 32, 128), sds(64, 48, 128), sds(64, 16, 128)
    dma = pltpu.SemaphoreType.DMA

    first, second = call(
        x_edges_kernel,
        (sds(576, 128), sds(576, 128)),
        (pressure, wind_east),
        buffers(*[(64, 8, 128)] * 4) + [dma((4,))],
        name="x_edges",
        specs={0: ANY, 1: ANY},
    )
    x2 = lax.ppermute(second, "gx", x_out)
    x1 = lax.ppermute(first, "gx", x_in)
    strip = call(y_edges_kernel, sds(12, 32, 128), (pressure, wind_north), name="y_edges")
    y1 = lax.ppermute(strip, "gy", y_in)
    y2 = lax.ppermute(strip, "gy", y_out)
    inv, g = call(coefficients_kernel, (field, field), (stiffness,), name="coefficients")

    def strips(value):
        rows = value.shape[2]
        value = value.reshape(3, 8, 8, rows, 3).transpose(1, 3, 2, 0, 4).reshape(8, rows, 8, 9)
        return jnp.pad(value, ((0, 0), (0, 0), (0, 0), (0, 7))).reshape(8, rows, 128)

    pe_strip = jnp.pad(strips(parent_east[:, :, :, :3]), ((0, 0), (0, 5), (0, 0)))
    pn_strip = jnp.concatenate([strips(parent_north), strips(parent_corner)], axis=1)
    pn_strip = jnp.pad(pn_strip, ((0, 0), (0, 5), (0, 0)))
    pe_rows = jnp.pad(parent_east, ((0, 0), (0, 0), (0, 5), (0, 0)))

    p1, u1, v1, vh1, rest = call(
        functools.partial(inner_kernel, True),
        (field, padded, field, field, outer),
        (pressure, wind_east, wind_north, inv, g, mat, y1, y2, pe_strip, pn_strip, pe_rows),
        buffers((64, 16, 128)),
        name="inner1",
        specs={8: ANY, 9: ANY, 10: ANY},
        us=3.0,
    )
    p1, u1, first, second = call(
        functools.partial(outer_kernel, True),
        (field, padded, sds(384, 128), sds(384, 128)),
        (x1, x2, pressure, wind_east, inv, g, rest, p1, u1),
        buffers(*[(64, 16, 128)] * 5),
        name="outer1",
        alias={7: 0, 8: 1},
    )
    x2 = lax.ppermute(second, "gx", x_out)
    x1 = lax.ppermute(first, "gx", x_in)
    strip = call(y_pack_kernel, sds(8, 32, 128), (p1,), name="y_pack")
    y1 = lax.ppermute(strip, "gy", y_in)
    y2 = lax.ppermute(strip, "gy", y_out)
    p2, u2, v2, rest = call(
        functools.partial(inner_kernel, False),
        (field, padded, field, outer),
        (p1, u1, v1, vh1, inv, g, mat, y1, y2),
        buffers((64, 16, 128)),
        name="inner2",
        us=3.0,
    )
    p2, u2, east = call(
        functools.partial(outer_kernel, False),
        (field, padded, sds(448, 128)),
        (x1, x2, p1, u1, inv, g, rest, p2, u2, v2, pn_strip),
        buffers(*[(64, 16, 128)] * 3),
        name="outer2",
        alias={7: 0, 8: 1},
    )
    down_x = [(i, (i - 1) % nx) for i in range(nx)]
    down_y = [(j, (j - 1) % ny) for j in range(ny)]
    down = [(i * ny + j, (i - 1) % nx * ny + (j - 1) % ny) for i in range(nx) for j in range(ny)]
    from_east = lax.ppermute(east, "gx", down_x)
    north = call(north_pack_kernel, sds(8, 40, 128), (u2, v2, p2, pe_strip), name="north_pack")
    from_north = lax.ppermute(north, "gy", down_y)
    from_both = lax.ppermute(north[:, :8, :], ("gx", "gy"), down)
    ru, rv, rp, tail = call(
        turn_kernel,
        (field, field, field, sds(3, 64, 8, 128)),
        (offsets, u2, v2, p2, pe_rows),
        name="turn",
        specs={0: SMEM},
        us=1.0,
    )
    return call(
        move_kernel,
        (field, field, field),
        (offsets, ru, rv, rp, tail, from_east, from_north, from_both, pn_strip),
        buffers(*[(64, 32, 128)] * 3, (3, 64, 16, 128), (8, 40, 128)) + [dma((24,))],
        name="move",
        specs={0: SMEM},
        outs=ANY,
    )


def solution(mesh):
    in_specs = (
        P(None, "gx", "gy"),
        P(None, "gx", "gy"),
        P(None, "gx", "gy"),
        P("gx", "gy"),
        P(None, None, None, "gy"),
        P(None, None, "gx", None),
        P(),
        P(),
    )
    out_specs = (P(None, "gx", "gy"), P(None, "gx", "gy"), P(None, "gx", "gy"))
    return jax.shard_map(
        on_device, mesh=mesh, in_specs=in_specs, out_specs=out_specs, check_vma=False
    )
```

```python
import functools

import jax
import jax.numpy as jnp
import numpy as np
from jax import lax
from jax.experimental import pallas as pl
from jax.experimental.pallas import tpu as pltpu
from jax.sharding import PartitionSpec as P

F32 = jnp.float32
BF16 = jnp.bfloat16

C1, C2, C3 = 0.45, 0.09, 0.01
CY = 0.01


def band():
    mat = np.zeros((256, 256), np.float32)
    for j in range(256):
        for k, w in ((1, 45.0), (2, -9.0), (3, 1.0)):
            mat[(j + k) % 256, j] = w
            mat[(j - k) % 256, j] = -w
    return mat


def swaps(count):
    inner = [(i, i ^ 1) for i in range(count)]
    outer = [(i, min(max(((i + 1) ^ 1) - 1, 0), count - 1)) for i in range(count)]
    return inner, outer


def lane_index():
    return lax.broadcasted_iota(jnp.int32, (1, 128), 1)


def roll_lanes(value, shift):
    return pltpu.roll(value, shift % 128, 1)


def dy(ext, mat):
    hi = ext.astype(BF16)
    lo = (ext - hi.astype(F32)).astype(BF16)
    return jnp.dot(hi, mat, preferred_element_type=F32) + jnp.dot(
        lo, mat, preferred_element_type=F32
    )


def pack(rows, width, step, lanes):
    out = None
    for m, row in enumerate(rows):
        moved = roll_lanes(row, m * step + width)
        out = moved if out is None else jnp.where(lanes >= m * step, moved, out)
    return out


def write_edges(buffers, east, first, second):
    def write(ref, side):
        at = 0
        for buf, width in buffers[side]:
            a = 0 if side == 0 else 8 - width
            for l in range(64):
                ref[at + width * l : at + width * (l + 1), :] = buf[l, a : a + width, :]
            at += 64 * width

    @pl.when(east)
    def _():
        write(first, 1)
        write(second, 0)

    @pl.when(jnp.logical_not(east))
    def _():
        write(first, 0)
        write(second, 1)


def x_edges_kernel(p, u, first, second, pw, pe, uw, ue, sems):
    copies = []
    for k, (src, buf, at) in enumerate(((p, pw, 0), (u, uw, 0), (p, pe, 24), (u, ue, 24))):
        copies.append(pltpu.make_async_copy(src.at[:, at : at + 8, :], buf, sems.at[k]))
    for copy in copies:
        copy.start()
    for copy in copies:
        copy.wait()
    even = lax.axis_index("gx") % 2 == 0
    write_edges((((pw, 6), (uw, 3)), ((pe, 6), (ue, 3))), even, first, second)


def y_edges_kernel(p, v, after, out):
    lanes = lane_index()
    for b in range(8):
        out[b] = pack([p[8 * b + m] for m in range(8)], 6, 16, lanes)
    for b in range(4):
        out[8 + b] = pack([v[16 * b + m] for m in range(16)], 3, 8, lanes)


def y_pack_kernel(p, out):
    lanes = lane_index()
    for b in range(8):
        out[b] = pack([p[8 * b + m] for m in range(8)], 6, 16, lanes)


def coefficients_kernel(s_ref, inv_ref, g_ref):
    s = s_ref[...]
    prev = None
    for l in range(64):
        if l == 0:
            div = 1.0 + s
        elif l < 63:
            div = 1.0 + 2.0 * s - s * prev
        else:
            div = 1.0 + s - s * prev
        inv = 1.0 / div
        inv_ref[l] = inv
        prev = s * inv
        g_ref[l] = prev


def difference(at):
    return C1 * (at(1) - at(-1)) - C2 * (at(2) - at(-2)) + C3 * (at(3) - at(-3))


def east_columns(out, field, pe, f):
    for l in range(64):
        out[3 * l : 3 * l + 3, :] = field[l, 0:3, :]

    @pl.when(lax.axis_index("gx") == 0)
    def _():
        for x in range(3):
            out[pl.ds(x, 64, stride=3), :] = pe[f, x]


def inner_kernel(first_step, p, u, v, *rest):
    if first_step:
        inv, g, mat, y1, y2, keep1, keep2, keep3, p_out, u_out, v_out, vh_out, rest_out, w_buf = rest
        du = 0
    else:
        vh_in, inv, g, mat, y1, y2, p_out, u_out, v_out, rest_out, w_buf = rest
        du = 8
    lanes = lane_index()
    gy = lax.axis_index("gy")
    even_y = gy % 2 == 0
    in_s = gy > 0
    in_n = gy < lax.axis_size("gy") - 1
    lane_ok = jnp.where(lanes < 64, jnp.where(in_n, 1.0, 0.0), jnp.where(in_s, 1.0, 0.0))

    def sides(b, low):
        a, c = y1[b], y2[b]
        north = jnp.where(in_n, jnp.where(even_y, a, c), 0.0)
        south = jnp.where(in_s, jnp.where(even_y, c, a), 0.0)
        return jnp.where(low, south, north)

    w = jnp.zeros((16, 128), F32)
    for b in range(8):
        blk = sides(b, lanes % 16 < 6)
        halo = jnp.concatenate([roll_lanes(blk, -(16 * m + 6)) for m in range(8)], axis=0)
        if first_step:
            blk = sides(8 + b // 2, lanes % 8 < 3)
            at = 64 * (b % 2) + 3
            vh = jnp.concatenate([roll_lanes(blk, -(at + 8 * m)) for m in range(8)], axis=0)
        else:
            vh = vh_in[8 * b : 8 * b + 8].reshape(256, 128)
        own = p[8 * b : 8 * b + 8].reshape(256, 128)
        d = dy(jnp.concatenate([own, halo], axis=1), mat[...])
        v1 = v[8 * b : 8 * b + 8].reshape(256, 128) - CY * d[:, :128]
        vh = (vh - CY * d[:, 128:]) * lane_ok
        v_out[8 * b : 8 * b + 8] = v1.reshape(8, 32, 128)
        if first_step:
            vh_out[8 * b : 8 * b + 8] = vh.reshape(8, 32, 128)
        d2 = dy(jnp.concatenate([v1, vh], axis=1), mat[:, :128])
        left = own - CY * d2
        for m in range(8):
            l = 8 * b + m
            row = left[32 * m : 32 * m + 32]
            rest_out[l, 0:8, :] = row[0:8]
            rest_out[l, 8:16, :] = row[24:32]
            step = difference(lambda k: p[l, 5 + k : 29 + k, :])
            u_out[l, 13:37, :] = u[l, du + 5 : du + 29, :] - step
            rhs = row[8:24] - difference(lambda k: u_out[l, 16 + k : 32 + k, :])
            w = rhs * inv[l, 8:24, :] + g[l, 8:24, :] * w
            w_buf[l] = w
    q = jnp.zeros((16, 128), F32)
    for l in range(63, -1, -1):
        q = w_buf[l] + g[l, 8:24, :] * q
        p_out[l, 8:24, :] = q


def outer_kernel(first_step, x1, x2, p, u, inv, g, rest, p_in, u_in, *tail):
    if first_step:
        p_out, u_out, first, second, pw, pe, uw, ue, w_buf = tail
    else:
        v, parent, p_out, u_out, east, pw, pe, w_buf = tail
    gx = lax.axis_index("gx")
    even = gx % 2 == 0
    in_w = gx > 0
    in_e = gx < lax.axis_size("gx") - 1

    def fill(ref, west):
        for l in range(64):
            part = jnp.where(in_w if west else in_e, ref[6 * l : 6 * l + 6, :], 0.0)
            if west:
                pw[l, 2:8, :] = part
            else:
                pe[l, 8:14, :] = part
            if first_step:
                part = ref[384 + 3 * l : 387 + 3 * l, :]
                if west:
                    uw[l, 5:8, :] = part
                else:
                    ue[l, 8:11, :] = part

    @pl.when(even)
    def _():
        fill(x1, False)
        fill(x2, True)

    @pl.when(jnp.logical_not(even))
    def _():
        fill(x1, True)
        fill(x2, False)

    rows = lax.broadcasted_iota(jnp.int32, (8, 128), 0)
    ok_w = jnp.where(rows < 3, jnp.where(in_w, 1.0, 0.0), 1.0)
    ok_e = jnp.where(rows >= 3, jnp.where(in_e, 1.0, 0.0), 1.0)
    w = jnp.zeros((16, 128), F32)
    for l in range(64):
        pw[l, 8:16, :] = p[l, 0:8, :]
        pe[l, 0:8, :] = p[l, 24:32, :]
        if first_step:
            uw[l, 8:16, :] = u[l, 0:8, :]
            ue[l, 0:8, :] = u[l, 24:32, :]
            old_w, old_e = uw[l, 5:13, :], ue[l, 5:13, :]
        else:
            old_w, old_e = u[l, 5:13, :], u[l, 37:45, :]
        u_out[l, 5:13, :] = (old_w - difference(lambda k: pw[l, 5 + k : 13 + k, :])) * ok_w
        u_out[l, 37:45, :] = (old_e - difference(lambda k: pe[l, 5 + k : 13 + k, :])) * ok_e
        rhs_w = rest[l, 0:8, :] - difference(lambda k: u_out[l, 8 + k : 16 + k, :])
        rhs_e = rest[l, 8:16, :] - difference(lambda k: u_out[l, 32 + k : 40 + k, :])
        rhs = jnp.concatenate([rhs_w, rhs_e], axis=0)
        il = jnp.concatenate([inv[l, 0:8, :], inv[l, 24:32, :]], axis=0)
        gl = jnp.concatenate([g[l, 0:8, :], g[l, 24:32, :]], axis=0)
        w = rhs * il + gl * w
        w_buf[l] = w
    q = jnp.zeros((16, 128), F32)
    for l in range(63, -1, -1):
        gl = jnp.concatenate([g[l, 0:8, :], g[l, 24:32, :]], axis=0)
        q = w_buf[l] + gl * q
        p_out[l, 0:8, :] = q[0:8]
        p_out[l, 24:32, :] = q[8:16]
        w_buf[l] = q
    if first_step:
        write_edges((((w_buf.at[:, 0:8, :], 6),), ((w_buf.at[:, 8:16, :], 6),)), even, first, second)
    else:
        east_columns(east.at[0:192], v, parent, 1)
        east_columns(east.at[192:384], w_buf, parent, 2)


def parents_kernel(pe, pn, pc, pe_strip, pn_strip, rows, cells):
    lanes = lane_index()
    for f in range(3):
        for x in range(3):
            rows[pl.ds(512 * f + x, 64, stride=8), :] = pe[f, x]
        for t in range(3):
            cells[3 * f + t, 0:32, 0:64] = pn[f, t]
            for x in range(3):
                cells[3 * f + t, 32 + x : 33 + x, 0:64] = pc[f, x, t : t + 1, :]
    lane = lax.broadcasted_iota(jnp.int32, (40, 128), 1)
    for b in range(8):
        strip = None
        for m in range(8):
            for f in range(3):
                at = 16 * m + 3 * f
                row = 512 * f + 8 * (8 * b + m)
                moved = roll_lanes(rows[row : row + 8, :], at)
                strip = moved if strip is None else jnp.where(lanes >= at, moved, strip)
        pe_strip[b] = strip
        strip = None
        for r in range(9):
            moved = jnp.take_along_axis(cells[r], 8 * b + lane // 16, axis=1, mode="promise_in_bounds")
            strip = moved if strip is None else jnp.where(lane % 16 >= r, moved, strip)
        pn_strip[b] = strip


def north_pack_kernel(u, v, p, pe, pn, out, out_corner):
    lanes = lane_index()
    west = lax.axis_index("gx") == 0
    south = lax.axis_index("gy") == 0
    for b in range(8):
        strip = None
        for m in range(8):
            l = 8 * b + m
            for f, val in enumerate((u[l, 8:40, :], v[l], p[l])):
                at = 16 * m + 3 * f
                moved = roll_lanes(val, at)
                strip = moved if strip is None else jnp.where(lanes >= at, moved, strip)
        out[b] = jnp.where(south, pn[b, 0:32, :], strip)
        edge = jnp.where(west, pn[b, 32:40, :], pn[b, 0:8, :])
        out_corner[b] = jnp.where(south, edge, jnp.where(west, pe[b], strip[0:8]))


def turn_kernel(offsets, u, v, p, pe, ru, rv, rp, tail):
    shift = lax.rem(128 - offsets[1], 128)
    for l in range(64):
        ru[l] = pltpu.roll(u[l, 8:40, :], shift, 1)
        rv[l] = pltpu.roll(v[l], shift, 1)
        rp[l] = pltpu.roll(p[l], shift, 1)
        tail[8 * l : 8 * l + 8, :] = pltpu.roll(u[l, 40:48, :], shift, 1)

    @pl.when(lax.axis_index("gx") == lax.axis_size("gx") - 1)
    def _():
        for x in range(3):
            tail[pl.ds(x, 64, stride=8), :] = pltpu.roll(pe[0, x], shift, 1)


def move_kernel(offsets, ru, rv, rp, tail, east, north, corner, ou, ov, op, bu, bv, bp, ext, ns, columns, sems):
    lanes = lane_index()
    o0, o1 = offsets[0], offsets[1]
    own_lane = lanes < 128 - o1
    shift = lax.rem(128 - o1, 128)
    columns[...] = pltpu.roll(east[...], shift, 1)
    copies = []
    for b in range(8):
        ns[b, 0:32, :] = north[b]
        ns[b, 32:40, :] = corner[b]
        nrow = ns[b, pl.ds(o0, 32), :]
        for m in range(8):
            l = 8 * b + m
            for f, (src, buf) in enumerate(((ru, bu), (rv, bv), (rp, bp))):
                ext[f, l, 0:8, :] = src[l, 24:32, :]
                if f == 0:
                    ext[f, l, 8:16, :] = tail[8 * l : 8 * l + 8, :]
                else:
                    at = 192 * (f - 1) + 3 * l
                    ext[f, l, 8:11, :] = columns[at : at + 3, :]
                back = lax.rem(256 - (16 * m + 3 * f) - o1, 128)
                strip = pltpu.roll(nrow, back, 1)
                buf[l, 0:24, :] = jnp.where(own_lane, src[l, pl.ds(o0, 24), :], strip[0:24])
                buf[l, 24:32, :] = jnp.where(own_lane, ext[f, l, pl.ds(o0, 8), :], strip[24:32])
        for f, (buf, out) in enumerate(((bu, ou), (bv, ov), (bp, op))):
            part = pl.ds(8 * b, 8)
            copy = pltpu.make_async_copy(buf.at[part], out.at[part], sems.at[8 * f + b])
            copy.start()
            copies.append(copy)
    for copy in copies:
        copy.wait()


VMEM = pl.BlockSpec(memory_space=pltpu.VMEM)
SMEM = pl.BlockSpec(memory_space=pltpu.SMEM)
ANY = pl.BlockSpec(memory_space=pl.ANY)
HBM = pl.BlockSpec(memory_space=pltpu.HBM)


def sds(*shape):
    return jax.ShapeDtypeStruct(shape, F32)


def buffers(*shapes):
    return [pltpu.VMEM(shape, F32) for shape in shapes]


def call(body, out_shape, args, scratch=(), name=None, specs=None, outs=None, alias=None, us=0.05, vmem=16):
    specs = {} if specs is None else specs
    return pl.pallas_call(
        body,
        out_shape=out_shape,
        in_specs=[specs.get(k, VMEM) for k in range(len(args))],
        out_specs=jax.tree.map(lambda _: outs or VMEM, out_shape),
        scratch_shapes=list(scratch),
        input_output_aliases=alias or {},
        name=name,
        cost_estimate=pl.CostEstimate(flops=0, bytes_accessed=int(us * 3.2e6), transcendentals=0),
        compiler_params=pltpu.CompilerParams(vmem_limit_bytes=vmem << 20),
    )(*args)


def on_device(wind_east, wind_north, pressure, stiffness, parent_east, parent_north, parent_corner, offsets):
    nx, ny = lax.axis_size("gx"), lax.axis_size("gy")
    mat = jnp.asarray(band(), BF16)
    x_in, x_out = swaps(nx)
    y_in, y_out = swaps(ny)
    field, padded, outer = sds(64, 32, 128), sds(64, 48, 128), sds(64, 16, 128)
    dma = pltpu.SemaphoreType.DMA

    first, second = call(
        x_edges_kernel,
        (sds(576, 128), sds(576, 128)),
        (pressure, wind_east),
        buffers(*[(64, 8, 128)] * 4) + [dma((4,))],
        name="x_edges",
        specs={0: HBM, 1: HBM},
        vmem=60,
    )
    x2 = lax.ppermute(second, "gx", x_out)
    x1 = lax.ppermute(first, "gx", x_in)
    strip = call(y_edges_kernel, sds(12, 32, 128), (pressure, wind_north, first), name="y_edges", specs={2: ANY})
    y1 = lax.ppermute(strip, "gy", y_in)
    y2 = lax.ppermute(strip, "gy", y_out)
    inv, g = call(coefficients_kernel, (field, field), (stiffness,), name="coefficients")

    pe = parent_east.transpose(0, 2, 1, 3)
    pe_strip, pn_strip = call(
        parents_kernel,
        (sds(8, 8, 128), sds(8, 40, 128)),
        (pe, parent_north.transpose(0, 3, 2, 1), parent_corner.transpose(0, 2, 3, 1)),
        buffers((3 * 64 * 8, 128), (9, 40, 128)),
        name="parents",
    )

    p1, u1, v1, vh1, rest = call(
        functools.partial(inner_kernel, True),
        (field, padded, field, field, outer),
        (pressure, wind_east, wind_north, inv, g, mat, y1, y2, pe_strip, pn_strip, pe),
        buffers((64, 16, 128)),
        name="inner1",
        specs={8: ANY, 9: ANY, 10: ANY},
        us=0.3,
    )
    p1, u1, first, second = call(
        functools.partial(outer_kernel, True),
        (field, padded, sds(384, 128), sds(384, 128)),
        (x1, x2, pressure, wind_east, inv, g, rest, p1, u1),
        buffers(*[(64, 16, 128)] * 5),
        name="outer1",
        alias={7: 0, 8: 1},
    )
    x2 = lax.ppermute(second, "gx", x_out)
    x1 = lax.ppermute(first, "gx", x_in)
    strip = call(y_pack_kernel, sds(8, 32, 128), (p1,), name="y_pack")
    y1 = lax.ppermute(strip, "gy", y_in)
    y2 = lax.ppermute(strip, "gy", y_out)
    p2, u2, v2, rest = call(
        functools.partial(inner_kernel, False),
        (field, padded, field, outer),
        (p1, u1, v1, vh1, inv, g, mat, y1, y2),
        buffers((64, 16, 128)),
        name="inner2",
        us=0.3,
    )
    down_x = [(i, (i - 1) % nx) for i in range(nx)]
    down_y = [(j, (j - 1) % ny) for j in range(ny)]
    down = [(i * ny + j, (i - 1) % nx * ny + (j - 1) % ny) for i in range(nx) for j in range(ny)]
    p2, u2, east = call(
        functools.partial(outer_kernel, False),
        (field, padded, sds(384, 128)),
        (x1, x2, p1, u1, inv, g, rest, p2, u2, v2, pe),
        buffers(*[(64, 16, 128)] * 3),
        name="outer2",
        alias={7: 0, 8: 1},
    )
    east = lax.ppermute(east, "gx", down_x)
    north, corner = call(
        north_pack_kernel,
        (sds(8, 32, 128), sds(8, 8, 128)),
        (u2, v2, p2, pe_strip, pn_strip),
        name="north_pack",
    )
    north = lax.ppermute(north, "gy", down_y)
    corner = lax.ppermute(corner, ("gx", "gy"), down)
    ru, rv, rp, tail = call(
        turn_kernel,
        (field, field, field, sds(512, 128)),
        (offsets, u2, v2, p2, pe),
        name="turn",
        specs={0: SMEM},
    )
    return call(
        move_kernel,
        (field, field, field),
        (offsets, ru, rv, rp, tail, east, north, corner),
        buffers(*[(64, 32, 128)] * 3, (3, 64, 16, 128), (8, 40, 128), (384, 128))
        + [dma((24,))],
        name="move",
        specs={0: SMEM},
        outs=ANY,
    )


def solution(mesh):
    in_specs = (
        P(None, "gx", "gy"),
        P(None, "gx", "gy"),
        P(None, "gx", "gy"),
        P("gx", "gy"),
        P(None, None, None, "gy"),
        P(None, None, "gx", None),
        P(),
        P(),
    )
    out_specs = (P(None, "gx", "gy"), P(None, "gx", "gy"), P(None, "gx", "gy"))
    return jax.shard_map(
        on_device, mesh=mesh, in_specs=in_specs, out_specs=out_specs, check_vma=False
    )
```

```python
import functools

import jax
import jax.numpy as jnp
import numpy as np
from jax import lax
from jax.experimental import pallas as pl
from jax.experimental.pallas import tpu as pltpu
from jax.sharding import PartitionSpec as P

F32 = jnp.float32
BF16 = jnp.bfloat16

C1, C2, C3 = 0.45, 0.09, 0.01
CY = 0.01


def band():
    mat = np.zeros((256, 256), np.float32)
    for j in range(256):
        for k, w in ((1, 45.0), (2, -9.0), (3, 1.0)):
            mat[(j + k) % 256, j] = w
            mat[(j - k) % 256, j] = -w
    return mat


def swaps(count):
    inner = [(i, i ^ 1) for i in range(count)]
    outer = [(i, (i + 1) % count if i % 2 else (i - 1) % count) for i in range(count)]
    return inner, outer


def lane_index():
    return lax.broadcasted_iota(jnp.int32, (1, 128), 1)


def roll_lanes(value, shift):
    return pltpu.roll(value, shift % 128, 1)


def dy(ext, mat):
    hi = ext.astype(BF16)
    lo = (ext - hi.astype(F32)).astype(BF16)
    return jnp.dot(hi, mat, preferred_element_type=F32) + jnp.dot(
        lo, mat, preferred_element_type=F32
    )


def pack_edges(rows, step, lanes):
    moved = [roll_lanes(row, m * step) for m, row in enumerate(rows)]
    low = high = moved[0]
    for m in range(1, len(moved)):
        low = jnp.where(lanes >= m * step, moved[m], low)
    for m in range(len(moved) - 1, 0, -1):
        high = jnp.where(lanes < m * step, moved[m], high)
    return low, high


def unpack_edges(north, south, m, step, lanes):
    mine = jnp.logical_and(lanes >= m * step, lanes < (m + 1) * step)
    return roll_lanes(jnp.where(mine, north, south), -m * step)


def write_edges(buffers, east, first, second):
    def write(ref, side):
        at = 0
        for buf, width in buffers[side]:
            a = 0 if side == 0 else 8 - width
            for l in range(64):
                ref[at + width * l : at + width * (l + 1), :] = buf[l, a : a + width, :]
            at += 64 * width

    @pl.when(east)
    def _():
        write(first, 1)
        write(second, 0)

    @pl.when(jnp.logical_not(east))
    def _():
        write(first, 0)
        write(second, 1)


def x_edges_kernel(p, u, first, second, pw, pe, uw, ue, sems):
    copies = []
    for k, (src, buf, at) in enumerate(((p, pw, 0), (u, uw, 0), (p, pe, 24), (u, ue, 24))):
        copies.append(pltpu.make_async_copy(src.at[:, at : at + 8, :], buf, sems.at[k]))
    for copy in copies:
        copy.start()
    for copy in copies:
        copy.wait()
    even = lax.axis_index("gx") % 2 == 0
    write_edges((((pw, 6), (uw, 3)), ((pe, 6), (ue, 3))), even, first, second)


def write_y_edges(field, count, step, at, first, second):
    lanes = lane_index()
    even = lax.axis_index("gy") % 2 == 0
    for b in range(64 // count):
        low, high = pack_edges([field[count * b + m] for m in range(count)], step, lanes)
        first[at + b] = jnp.where(even, high, low)
        second[at + b] = jnp.where(even, low, high)


def y_edges_kernel(p, v, first, second):
    write_y_edges(p, 16, 8, 0, first, second)
    write_y_edges(v, 32, 4, 4, first, second)


def y_pack_kernel(p, first, second):
    write_y_edges(p, 16, 8, 0, first, second)


def coefficients_kernel(s_ref, inv_ref, g_ref):
    s = s_ref[...]
    prev = None
    for l in range(64):
        if l == 0:
            div = 1.0 + s
        elif l < 63:
            div = 1.0 + 2.0 * s - s * prev
        else:
            div = 1.0 + s - s * prev
        inv = 1.0 / div
        inv_ref[l] = inv
        prev = s * inv
        g_ref[l] = prev


def difference(at):
    return C1 * (at(1) - at(-1)) - C2 * (at(2) - at(-2)) + C3 * (at(3) - at(-3))


def east_columns(out, field, pe, f):
    for l in range(64):
        out[3 * l : 3 * l + 3, :] = field[l, 0:3, :]

    @pl.when(lax.axis_index("gx") == 0)
    def _():
        for x in range(3):
            out[pl.ds(x, 64, stride=3), :] = pe[f, x]


def across_kernel(first_step, p, u, u_out, ex_out):
    du = 0 if first_step else 8
    for l in range(64):
        step = difference(lambda k: p[l, 5 + k : 29 + k, :])
        u_out[l, 13:37, :] = u[l, du + 5 : du + 29, :] - step
        ex_out[l] = difference(lambda k: u_out[l, 16 + k : 32 + k, :])


def inner_kernel(first_step, p, v, ex, *rest):
    if first_step:
        inv, g, mat, y1, y2, keep1, keep2, keep3, p_out, v_out, vh_out, rest_out, w_buf = rest
    else:
        vh_in, inv, g, mat, y1, y2, p_out, v_out, rest_out, w_buf = rest
    lanes = lane_index()
    gy = lax.axis_index("gy")
    even_y = gy % 2 == 0
    in_s = gy > 0
    in_n = gy < lax.axis_size("gy") - 1
    lane_ok = jnp.where(lanes < 64, jnp.where(in_n, 1.0, 0.0), jnp.where(in_s, 1.0, 0.0))

    def halos(at, levels, count, step):
        out = []
        for l in levels:
            a, c = y1[at + l // count], y2[at + l // count]
            north = jnp.where(in_n, jnp.where(even_y, a, c), 0.0)
            south = jnp.where(in_s, jnp.where(even_y, c, a), 0.0)
            out.append(unpack_edges(north, south, l % count, step, lanes))
        return jnp.concatenate(out, axis=0)

    w = jnp.zeros((16, 128), F32)
    for b in range(8):
        levels = range(8 * b, 8 * b + 8)
        halo = halos(0, levels, 16, 8)
        if first_step:
            vh = halos(4, levels, 32, 4)
        else:
            vh = vh_in[8 * b : 8 * b + 8].reshape(256, 128)
        own = p[8 * b : 8 * b + 8].reshape(256, 128)
        d = dy(jnp.concatenate([own, halo], axis=1), mat[...])
        v1 = v[8 * b : 8 * b + 8].reshape(256, 128) - CY * d[:, :128]
        vh = (vh - CY * d[:, 128:]) * lane_ok
        v_out[8 * b : 8 * b + 8] = v1.reshape(8, 32, 128)
        if first_step:
            vh_out[8 * b : 8 * b + 8] = vh.reshape(8, 32, 128)
        d2 = dy(jnp.concatenate([v1, vh], axis=1), mat[:, :128])
        left = own - CY * d2
        for m in range(8):
            l = 8 * b + m
            row = left[32 * m : 32 * m + 32]
            rest_out[l, 0:8, :] = row[0:8]
            rest_out[l, 8:16, :] = row[24:32]
            w = (row[8:24] - ex[l]) * inv[l, 8:24, :] + g[l, 8:24, :] * w
            w_buf[l] = w
    q = jnp.zeros((16, 128), F32)
    for l in range(63, -1, -1):
        q = w_buf[l] + g[l, 8:24, :] * q
        p_out[l, 8:24, :] = q


def outer_kernel(first_step, x1, x2, p, u, inv, g, rest, p_in, u_in, *tail):
    if first_step:
        p_out, u_out, first, second, pw, pe, uw, ue, w_buf = tail
    else:
        v, parent, p_out, u_out, east, pw, pe, w_buf = tail
    gx = lax.axis_index("gx")
    even = gx % 2 == 0
    in_w = gx > 0
    in_e = gx < lax.axis_size("gx") - 1

    def fill(ref, west):
        for l in range(64):
            part = jnp.where(in_w if west else in_e, ref[6 * l : 6 * l + 6, :], 0.0)
            if west:
                pw[l, 2:8, :] = part
            else:
                pe[l, 8:14, :] = part
            if first_step:
                part = ref[384 + 3 * l : 387 + 3 * l, :]
                if west:
                    uw[l, 5:8, :] = part
                else:
                    ue[l, 8:11, :] = part

    @pl.when(even)
    def _():
        fill(x1, False)
        fill(x2, True)

    @pl.when(jnp.logical_not(even))
    def _():
        fill(x1, True)
        fill(x2, False)

    rows = lax.broadcasted_iota(jnp.int32, (8, 128), 0)
    ok_w = jnp.where(rows < 3, jnp.where(in_w, 1.0, 0.0), 1.0)
    ok_e = jnp.where(rows >= 3, jnp.where(in_e, 1.0, 0.0), 1.0)
    w = jnp.zeros((16, 128), F32)
    for l in range(64):
        pw[l, 8:16, :] = p[l, 0:8, :]
        pe[l, 0:8, :] = p[l, 24:32, :]
        if first_step:
            uw[l, 8:16, :] = u[l, 0:8, :]
            ue[l, 0:8, :] = u[l, 24:32, :]
            old_w, old_e = uw[l, 5:13, :], ue[l, 5:13, :]
        else:
            old_w, old_e = u[l, 5:13, :], u[l, 37:45, :]
        u_out[l, 5:13, :] = (old_w - difference(lambda k: pw[l, 5 + k : 13 + k, :])) * ok_w
        u_out[l, 37:45, :] = (old_e - difference(lambda k: pe[l, 5 + k : 13 + k, :])) * ok_e
        rhs_w = rest[l, 0:8, :] - difference(lambda k: u_out[l, 8 + k : 16 + k, :])
        rhs_e = rest[l, 8:16, :] - difference(lambda k: u_out[l, 32 + k : 40 + k, :])
        rhs = jnp.concatenate([rhs_w, rhs_e], axis=0)
        il = jnp.concatenate([inv[l, 0:8, :], inv[l, 24:32, :]], axis=0)
        gl = jnp.concatenate([g[l, 0:8, :], g[l, 24:32, :]], axis=0)
        w = rhs * il + gl * w
        w_buf[l] = w
    q = jnp.zeros((16, 128), F32)
    for l in range(63, -1, -1):
        gl = jnp.concatenate([g[l, 0:8, :], g[l, 24:32, :]], axis=0)
        q = w_buf[l] + gl * q
        p_out[l, 0:8, :] = q[0:8]
        p_out[l, 24:32, :] = q[8:16]
        w_buf[l] = q
    if first_step:
        write_edges((((w_buf.at[:, 0:8, :], 6),), ((w_buf.at[:, 8:16, :], 6),)), even, first, second)
    else:
        east_columns(east.at[0:192], v, parent, 1)
        east_columns(east.at[192:384], w_buf, parent, 2)


def parents_kernel(pe, pn, pc, pe_strip, pn_strip, rows, cells):
    lanes = lane_index()
    for f in range(3):
        for x in range(3):
            rows[pl.ds(512 * f + x, 64, stride=8), :] = pe[f, x]
        for t in range(3):
            cells[3 * f + t, 0:32, 0:64] = pn[f, t]
            for x in range(3):
                cells[3 * f + t, 32 + x : 33 + x, 0:64] = pc[f, x, t : t + 1, :]
    lane = lax.broadcasted_iota(jnp.int32, (40, 128), 1)
    for b in range(8):
        strip = None
        for m in range(8):
            for f in range(3):
                at = 16 * m + 3 * f
                row = 512 * f + 8 * (8 * b + m)
                moved = roll_lanes(rows[row : row + 8, :], at)
                strip = moved if strip is None else jnp.where(lanes >= at, moved, strip)
        pe_strip[b] = strip
        strip = None
        for r in range(9):
            moved = jnp.take_along_axis(cells[r], 8 * b + lane // 16, axis=1, mode="promise_in_bounds")
            strip = moved if strip is None else jnp.where(lane % 16 >= r, moved, strip)
        pn_strip[b] = strip


def strip_of(fields, b, lanes):
    strip = None
    for m in range(8):
        for f, field in enumerate(fields):
            moved = roll_lanes(field(8 * b + m), 16 * m + 3 * f)
            strip = moved if strip is None else jnp.where(lanes >= 16 * m + 3 * f, moved, strip)
    return strip


def corner_pack_kernel(u, v, p, pe, pn, out):
    lanes = lane_index()
    west = lax.axis_index("gx") == 0
    south = lax.axis_index("gy") == 0
    fields = (lambda l: u[l, 8:16, :], lambda l: v[l, 0:8, :], lambda l: p[l, 0:8, :])
    for b in range(8):
        edge = jnp.where(west, pn[b, 32:40, :], pn[b, 0:8, :])
        strip = strip_of(fields, b, lanes)
        out[b] = jnp.where(south, edge, jnp.where(west, pe[b], strip))


def north_pack_kernel(u, v, p, pn, after, out):
    lanes = lane_index()
    south = lax.axis_index("gy") == 0
    fields = (lambda l: u[l, 8:40, :], lambda l: v[l], lambda l: p[l])
    for b in range(8):
        out[b] = jnp.where(south, pn[b, 0:32, :], strip_of(fields, b, lanes))


def turn_kernel(offsets, u, v, p, pe, ru, rv, rp, tu, tv, tp):
    o0 = offsets[0]
    shift = lax.rem(128 - offsets[1], 128)
    for l in range(64):
        tu[40 * l : 40 * l + 40, :] = pltpu.roll(u[l, 8:48, :], shift, 1)
        tv[40 * l : 40 * l + 32, :] = pltpu.roll(v[l], shift, 1)
        tp[40 * l : 40 * l + 32, :] = pltpu.roll(p[l], shift, 1)

    @pl.when(lax.axis_index("gx") == lax.axis_size("gx") - 1)
    def _():
        for x in range(3):
            tu[pl.ds(32 + x, 64, stride=40), :] = pltpu.roll(pe[0, x], shift, 1)

    for l in range(64):
        ru[l] = tu[pl.ds(40 * l + o0, 32), :]
        rv[l] = tv[pl.ds(40 * l + o0, 32), :]
        rp[l] = tp[pl.ds(40 * l + o0, 32), :]


def move_kernel(offsets, ru, rv, rp, east, north, corner, ou, ov, op, bu, bv, bp, ns, columns, sems):
    lanes = lane_index()
    o0, o1 = offsets[0], offsets[1]
    own_lane = lanes < 128 - o1
    own_row = lax.broadcasted_iota(jnp.int32, (8, 128), 0) < 8 - o0
    shift = lax.rem(128 - o1, 128)
    columns[8:392, :] = pltpu.roll(east[...], shift, 1)
    copies = []
    for b in range(8):
        ns[b, 0:32, :] = north[b]
        ns[b, 32:40, :] = corner[b]
        nrow = ns[b, pl.ds(o0, 32), :]
        for m in range(8):
            l = 8 * b + m
            for f, (src, buf) in enumerate(((ru, bu), (rv, bv), (rp, bp))):
                back = lax.rem(256 - (16 * m + 3 * f) - o1, 128)
                strip = pltpu.roll(nrow, back, 1)
                buf[l, 0:24, :] = jnp.where(own_lane, src[l, 0:24, :], strip[0:24])
                last = src[l, 24:32, :]
                if f > 0:
                    new = columns[pl.ds(192 * (f - 1) + 3 * l + o0, 8), :]
                    last = jnp.where(own_row, last, new)
                buf[l, 24:32, :] = jnp.where(own_lane, last, strip[24:32])
        for f, (buf, out) in enumerate(((bu, ou), (bv, ov), (bp, op))):
            part = pl.ds(8 * b, 8)
            copy = pltpu.make_async_copy(buf.at[part], out.at[part], sems.at[8 * f + b])
            copy.start()
            copies.append(copy)
    for copy in copies:
        copy.wait()


VMEM = pl.BlockSpec(memory_space=pltpu.VMEM)
SMEM = pl.BlockSpec(memory_space=pltpu.SMEM)
ANY = pl.BlockSpec(memory_space=pl.ANY)
HBM = pl.BlockSpec(memory_space=pltpu.HBM)


def sds(*shape):
    return jax.ShapeDtypeStruct(shape, F32)


def buffers(*shapes):
    return [pltpu.VMEM(shape, F32) for shape in shapes]


def call(body, out_shape, args, scratch=(), name=None, specs=None, outs=None, alias=None, us=0.05, vmem=16):
    specs = {} if specs is None else specs
    return pl.pallas_call(
        body,
        out_shape=out_shape,
        in_specs=[specs.get(k, VMEM) for k in range(len(args))],
        out_specs=jax.tree.map(lambda _: outs or VMEM, out_shape),
        scratch_shapes=list(scratch),
        input_output_aliases=alias or {},
        name=name,
        cost_estimate=pl.CostEstimate(flops=0, bytes_accessed=int(us * 3.2e6), transcendentals=0),
        compiler_params=pltpu.CompilerParams(vmem_limit_bytes=vmem << 20),
    )(*args)


def on_device(wind_east, wind_north, pressure, stiffness, parent_east, parent_north, parent_corner, offsets):
    nx, ny = lax.axis_size("gx"), lax.axis_size("gy")
    mat = jnp.asarray(band(), BF16)
    x_in, x_out = swaps(nx)
    y_in, y_out = swaps(ny)
    field, padded, outer = sds(64, 32, 128), sds(64, 48, 128), sds(64, 16, 128)
    dma = pltpu.SemaphoreType.DMA

    first, second = call(
        x_edges_kernel,
        (sds(576, 128), sds(576, 128)),
        (pressure, wind_east),
        buffers(*[(64, 8, 128)] * 4) + [dma((4,))],
        name="x_edges",
        specs={0: HBM, 1: HBM},
        vmem=60,
    )
    x2 = lax.ppermute(second, "gx", x_out)
    x1 = lax.ppermute(first, "gx", x_in)
    first, second = call(
        y_edges_kernel, (sds(6, 32, 128), sds(6, 32, 128)), (pressure, wind_north), name="y_edges"
    )
    y1 = lax.ppermute(first, "gy", y_in)
    y2 = lax.ppermute(second, "gy", y_out)
    inv, g = call(coefficients_kernel, (field, field), (stiffness,), name="coefficients")

    pe = parent_east.transpose(0, 2, 1, 3)
    pe_strip, pn_strip = call(
        parents_kernel,
        (sds(8, 8, 128), sds(8, 40, 128)),
        (pe, parent_north.transpose(0, 3, 2, 1), parent_corner.transpose(0, 2, 3, 1)),
        buffers((3 * 64 * 8, 128), (9, 40, 128)),
        name="parents",
    )

    u1, ex = call(
        functools.partial(across_kernel, True), (padded, outer), (pressure, wind_east), name="across1"
    )
    p1, v1, vh1, rest = call(
        functools.partial(inner_kernel, True),
        (field, field, field, outer),
        (pressure, wind_north, ex, inv, g, mat, y1, y2, pe_strip, pn_strip, pe),
        buffers((64, 16, 128)),
        name="inner1",
        specs={8: ANY, 9: ANY, 10: ANY},
        us=0.3,
    )
    p1, u1, first, second = call(
        functools.partial(outer_kernel, True),
        (field, padded, sds(384, 128), sds(384, 128)),
        (x1, x2, pressure, wind_east, inv, g, rest, p1, u1),
        buffers(*[(64, 16, 128)] * 5),
        name="outer1",
        alias={7: 0, 8: 1},
    )
    x2 = lax.ppermute(second, "gx", x_out)
    x1 = lax.ppermute(first, "gx", x_in)
    first, second = call(
        y_pack_kernel, (sds(4, 32, 128), sds(4, 32, 128)), (p1,), name="y_pack"
    )
    y1 = lax.ppermute(first, "gy", y_in)
    y2 = lax.ppermute(second, "gy", y_out)
    u2, ex = call(
        functools.partial(across_kernel, False), (padded, outer), (p1, u1), name="across2"
    )
    p2, v2, rest = call(
        functools.partial(inner_kernel, False),
        (field, field, outer),
        (p1, v1, ex, vh1, inv, g, mat, y1, y2),
        buffers((64, 16, 128)),
        name="inner2",
        us=0.3,
    )
    down_x = [(i, (i - 1) % nx) for i in range(nx)]
    down_y = [(j, (j - 1) % ny) for j in range(ny)]
    down = [(i * ny + j, (i - 1) % nx * ny + (j - 1) % ny) for i in range(nx) for j in range(ny)]
    p2, u2, east = call(
        functools.partial(outer_kernel, False),
        (field, padded, sds(384, 128)),
        (x1, x2, p1, u1, inv, g, rest, p2, u2, v2, pe),
        buffers(*[(64, 16, 128)] * 3),
        name="outer2",
        alias={7: 0, 8: 1},
    )
    east = lax.ppermute(east, "gx", down_x)
    corner = call(
        corner_pack_kernel, sds(8, 8, 128), (u2, v2, p2, pe_strip, pn_strip), name="corner_pack"
    )
    from_corner = lax.ppermute(corner, ("gx", "gy"), down)
    north = call(
        north_pack_kernel, sds(8, 32, 128), (u2, v2, p2, pn_strip, corner), name="north_pack"
    )
    north = lax.ppermute(north, "gy", down_y)
    ru, rv, rp = call(
        turn_kernel,
        (field, field, field),
        (offsets, u2, v2, p2, pe),
        buffers(*[(64 * 40, 128)] * 3),
        name="turn",
        specs={0: SMEM},
    )
    return call(
        move_kernel,
        (field, field, field),
        (offsets, ru, rv, rp, east, north, from_corner),
        buffers(*[(64, 32, 128)] * 3, (8, 40, 128), (392, 128))
        + [dma((24,))],
        name="move",
        specs={0: SMEM},
        outs=ANY,
    )


def solution(mesh):
    in_specs = (
        P(None, "gx", "gy"),
        P(None, "gx", "gy"),
        P(None, "gx", "gy"),
        P("gx", "gy"),
        P(None, None, None, "gy"),
        P(None, None, "gx", None),
        P(),
        P(),
    )
    out_specs = (P(None, "gx", "gy"), P(None, "gx", "gy"), P(None, "gx", "gy"))
    return jax.shard_map(
        on_device, mesh=mesh, in_specs=in_specs, out_specs=out_specs, check_vma=False
    )
```

```python
import functools

import jax
import jax.numpy as jnp
import numpy as np
from jax import lax
from jax.experimental import pallas as pl
from jax.experimental.pallas import tpu as pltpu
from jax.sharding import PartitionSpec as P

F32 = jnp.float32
BF16 = jnp.bfloat16

C1, C2, C3 = 0.45, 0.09, 0.01
CY = 0.01


def band():
    mat = np.zeros((256, 256), np.float32)
    for j in range(256):
        for k, w in ((1, 45.0), (2, -9.0), (3, 1.0)):
            mat[(j + k) % 256, j] = w
            mat[(j - k) % 256, j] = -w
    return mat


def swaps(count):
    inner = [(i, i ^ 1) for i in range(count)]
    outer = [(i, (i + 1) % count if i % 2 else (i - 1) % count) for i in range(count)]
    return inner, outer


def lane_index():
    return lax.broadcasted_iota(jnp.int32, (1, 128), 1)


def roll_lanes(value, shift):
    return pltpu.roll(value, shift % 128, 1)


def dy(ext, mat):
    hi = ext.astype(BF16)
    lo = (ext - hi.astype(F32)).astype(BF16)
    both = jnp.dot(jnp.concatenate([hi, lo], axis=0), mat, preferred_element_type=F32)
    return both[: ext.shape[0]] + both[ext.shape[0] :]


def pack_edges(rows, step, lanes):
    moved = [roll_lanes(row, m * step) for m, row in enumerate(rows)]
    low = high = moved[0]
    for m in range(1, len(moved)):
        low = jnp.where(lanes >= m * step, moved[m], low)
    for m in range(len(moved) - 1, 0, -1):
        high = jnp.where(lanes < m * step, moved[m], high)
    return low, high


def unpack_edges(north, south, m, step, lanes):
    mine = jnp.logical_and(lanes >= m * step, lanes < (m + 1) * step)
    return roll_lanes(jnp.where(mine, north, south), -m * step)


def write_edges(buffers, east, first, second):
    def write(ref, side):
        at = 0
        for buf, width in buffers[side]:
            a = 0 if side == 0 else 8 - width
            for l in range(64):
                ref[at + width * l : at + width * (l + 1), :] = buf[l, a : a + width, :]
            at += 64 * width

    @pl.when(east)
    def _():
        write(first, 1)
        write(second, 0)

    @pl.when(jnp.logical_not(east))
    def _():
        write(first, 0)
        write(second, 1)


def x_edges_kernel(p, u, first, second, pw, pe, uw, ue, sems):
    copies = []
    for k, (src, buf, at) in enumerate(((p, pw, 0), (u, uw, 0), (p, pe, 24), (u, ue, 24))):
        copies.append(pltpu.make_async_copy(src.at[:, at : at + 8, :], buf, sems.at[k]))
    for copy in copies:
        copy.start()
    for copy in copies:
        copy.wait()
    even = lax.axis_index("gx") % 2 == 0
    write_edges((((pw, 6), (uw, 3)), ((pe, 6), (ue, 3))), even, first, second)


def write_y_edges(field, count, step, at, first, second):
    lanes = lane_index()
    even = lax.axis_index("gy") % 2 == 0
    for b in range(64 // count):
        low, high = pack_edges([field[count * b + m] for m in range(count)], step, lanes)
        first[at + b] = jnp.where(even, high, low)
        second[at + b] = jnp.where(even, low, high)


def y_edges_kernel(p, v, first, second):
    write_y_edges(p, 16, 8, 0, first, second)
    write_y_edges(v, 32, 4, 4, first, second)


def y_pack_kernel(p, first, second):
    write_y_edges(p, 16, 8, 0, first, second)


def coefficients_kernel(s_ref, inv_ref, g_ref):
    s = s_ref[...]
    prev = None
    for l in range(64):
        if l == 0:
            div = 1.0 + s
        elif l < 63:
            div = 1.0 + 2.0 * s - s * prev
        else:
            div = 1.0 + s - s * prev
        inv = 1.0 / div
        inv_ref[l] = inv
        prev = s * inv
        g_ref[l] = prev


def difference(at):
    return C1 * (at(1) - at(-1)) - C2 * (at(2) - at(-2)) + C3 * (at(3) - at(-3))


def east_columns(out, field, pe, f):
    for l in range(64):
        out[3 * l : 3 * l + 3, :] = field[l, 0:3, :]

    @pl.when(lax.axis_index("gx") == 0)
    def _():
        for x in range(3):
            out[pl.ds(x, 64, stride=3), :] = pe[f, x]


def across_kernel(first_step, p, u, u_out, ex_out):
    du = 0 if first_step else 8
    for l in range(64):
        step = difference(lambda k: p[l, 5 + k : 29 + k, :])
        u_out[l, 13:37, :] = u[l, du + 5 : du + 29, :] - step
        ex_out[l] = difference(lambda k: u_out[l, 16 + k : 32 + k, :])


def inner_kernel(first_step, p, v, ex, *rest):
    if first_step:
        inv, g, mat, y1, y2, keep1, keep2, keep3, p_out, v_out, vh_out, rest_out, w_buf = rest
    else:
        vh_in, inv, g, mat, y1, y2, p_out, v_out, rest_out, w_buf = rest
    lanes = lane_index()
    gy = lax.axis_index("gy")
    even_y = gy % 2 == 0
    in_s = gy > 0
    in_n = gy < lax.axis_size("gy") - 1
    lane_ok = jnp.where(lanes < 64, jnp.where(in_n, 1.0, 0.0), jnp.where(in_s, 1.0, 0.0))

    def halos(at, levels, count, step):
        out = []
        for l in levels:
            a, c = y1[at + l // count], y2[at + l // count]
            north = jnp.where(in_n, jnp.where(even_y, a, c), 0.0)
            south = jnp.where(in_s, jnp.where(even_y, c, a), 0.0)
            out.append(unpack_edges(north, south, l % count, step, lanes))
        return jnp.concatenate(out, axis=0)

    w = jnp.zeros((16, 128), F32)
    for b in range(8):
        levels = range(8 * b, 8 * b + 8)
        halo = halos(0, levels, 16, 8)
        if first_step:
            vh = halos(4, levels, 32, 4)
        else:
            vh = vh_in[8 * b : 8 * b + 8].reshape(256, 128)
        own = p[8 * b : 8 * b + 8].reshape(256, 128)
        d = dy(jnp.concatenate([own, halo], axis=1), mat[...])
        v1 = v[8 * b : 8 * b + 8].reshape(256, 128) - CY * d[:, :128]
        vh = (vh - CY * d[:, 128:]) * lane_ok
        v_out[8 * b : 8 * b + 8] = v1.reshape(8, 32, 128)
        if first_step:
            vh_out[8 * b : 8 * b + 8] = vh.reshape(8, 32, 128)
        d2 = dy(jnp.concatenate([v1, vh], axis=1), mat[:, :128])
        left = own - CY * d2
        for m in range(8):
            l = 8 * b + m
            row = left[32 * m : 32 * m + 32]
            rest_out[l, 0:8, :] = row[0:8]
            rest_out[l, 8:16, :] = row[24:32]
            w = (row[8:24] - ex[l]) * inv[l, 8:24, :] + g[l, 8:24, :] * w
            w_buf[l] = w
    q = jnp.zeros((16, 128), F32)
    for l in range(63, -1, -1):
        q = w_buf[l] + g[l, 8:24, :] * q
        p_out[l, 8:24, :] = q


def outer_kernel(first_step, x1, x2, p, u, inv, g, rest, p_in, u_in, *tail):
    if first_step:
        p_out, u_out, first, second, pw, pe, uw, ue, w_buf = tail
    else:
        v, parent, p_out, u_out, east, pw, pe, w_buf = tail
    gx = lax.axis_index("gx")
    even = gx % 2 == 0
    in_w = gx > 0
    in_e = gx < lax.axis_size("gx") - 1

    def fill(ref, west):
        for l in range(64):
            part = jnp.where(in_w if west else in_e, ref[6 * l : 6 * l + 6, :], 0.0)
            if west:
                pw[l, 2:8, :] = part
            else:
                pe[l, 8:14, :] = part
            if first_step:
                part = ref[384 + 3 * l : 387 + 3 * l, :]
                if west:
                    uw[l, 5:8, :] = part
                else:
                    ue[l, 8:11, :] = part

    @pl.when(even)
    def _():
        fill(x1, False)
        fill(x2, True)

    @pl.when(jnp.logical_not(even))
    def _():
        fill(x1, True)
        fill(x2, False)

    rows = lax.broadcasted_iota(jnp.int32, (8, 128), 0)
    ok_w = jnp.where(rows < 3, jnp.where(in_w, 1.0, 0.0), 1.0)
    ok_e = jnp.where(rows >= 3, jnp.where(in_e, 1.0, 0.0), 1.0)
    w = jnp.zeros((16, 128), F32)
    for l in range(64):
        pw[l, 8:16, :] = p[l, 0:8, :]
        pe[l, 0:8, :] = p[l, 24:32, :]
        if first_step:
            uw[l, 8:16, :] = u[l, 0:8, :]
            ue[l, 0:8, :] = u[l, 24:32, :]
            old_w, old_e = uw[l, 5:13, :], ue[l, 5:13, :]
        else:
            old_w, old_e = u[l, 5:13, :], u[l, 37:45, :]
        u_out[l, 5:13, :] = (old_w - difference(lambda k: pw[l, 5 + k : 13 + k, :])) * ok_w
        u_out[l, 37:45, :] = (old_e - difference(lambda k: pe[l, 5 + k : 13 + k, :])) * ok_e
        rhs_w = rest[l, 0:8, :] - difference(lambda k: u_out[l, 8 + k : 16 + k, :])
        rhs_e = rest[l, 8:16, :] - difference(lambda k: u_out[l, 32 + k : 40 + k, :])
        rhs = jnp.concatenate([rhs_w, rhs_e], axis=0)
        il = jnp.concatenate([inv[l, 0:8, :], inv[l, 24:32, :]], axis=0)
        gl = jnp.concatenate([g[l, 0:8, :], g[l, 24:32, :]], axis=0)
        w = rhs * il + gl * w
        w_buf[l] = w
    q = jnp.zeros((16, 128), F32)
    for l in range(63, -1, -1):
        gl = jnp.concatenate([g[l, 0:8, :], g[l, 24:32, :]], axis=0)
        q = w_buf[l] + gl * q
        p_out[l, 0:8, :] = q[0:8]
        p_out[l, 24:32, :] = q[8:16]
        w_buf[l] = q
    if first_step:
        write_edges((((w_buf.at[:, 0:8, :], 6),), ((w_buf.at[:, 8:16, :], 6),)), even, first, second)
    else:
        east_columns(east.at[0:192], v, parent, 1)
        east_columns(east.at[192:384], w_buf, parent, 2)


def parents_kernel(pe, pn, pc, pe_strip, pn_strip, rows, cells):
    lanes = lane_index()
    for f in range(3):
        for x in range(3):
            rows[pl.ds(512 * f + x, 64, stride=8), :] = pe[f, x]
        for t in range(3):
            cells[3 * f + t, 0:32, 0:64] = pn[f, t]
            for x in range(3):
                cells[3 * f + t, 32 + x : 33 + x, 0:64] = pc[f, x, t : t + 1, :]
    lane = lax.broadcasted_iota(jnp.int32, (40, 128), 1)
    for b in range(8):
        strip = None
        for m in range(8):
            for f in range(3):
                at = 16 * m + 3 * f
                row = 512 * f + 8 * (8 * b + m)
                moved = roll_lanes(rows[row : row + 8, :], at)
                strip = moved if strip is None else jnp.where(lanes >= at, moved, strip)
        pe_strip[b] = strip
        strip = None
        for r in range(9):
            moved = jnp.take_along_axis(cells[r], 8 * b + lane // 16, axis=1, mode="promise_in_bounds")
            strip = moved if strip is None else jnp.where(lane % 16 >= r, moved, strip)
        pn_strip[b] = strip


def strip_of(fields, b, lanes):
    strip = None
    for m in range(8):
        for f, field in enumerate(fields):
            moved = roll_lanes(field(8 * b + m), 16 * m + 3 * f)
            strip = moved if strip is None else jnp.where(lanes >= 16 * m + 3 * f, moved, strip)
    return strip


def corner_pack_kernel(u, v, p, pe, pn, out):
    lanes = lane_index()
    west = lax.axis_index("gx") == 0
    south = lax.axis_index("gy") == 0
    fields = (lambda l: u[l, 8:16, :], lambda l: v[l, 0:8, :], lambda l: p[l, 0:8, :])
    for b in range(8):
        edge = jnp.where(west, pn[b, 32:40, :], pn[b, 0:8, :])
        strip = strip_of(fields, b, lanes)
        out[b] = jnp.where(south, edge, jnp.where(west, pe[b], strip))


def north_pack_kernel(u, v, p, pn, after, out):
    lanes = lane_index()
    south = lax.axis_index("gy") == 0
    fields = (lambda l: u[l, 8:40, :], lambda l: v[l], lambda l: p[l])
    for b in range(8):
        out[b] = jnp.where(south, pn[b, 0:32, :], strip_of(fields, b, lanes))


def turn_kernel(offsets, u, v, p, pe, ru, rv, rp, tu, tv, tp):
    o0 = offsets[0, 0]
    shift = lax.rem(128 - offsets[0, 1], 128)
    for l in range(64):
        tu[40 * l : 40 * l + 40, :] = pltpu.roll(u[l, 8:48, :], shift, 1)
        tv[40 * l : 40 * l + 32, :] = pltpu.roll(v[l], shift, 1)
        tp[40 * l : 40 * l + 32, :] = pltpu.roll(p[l], shift, 1)

    @pl.when(lax.axis_index("gx") == lax.axis_size("gx") - 1)
    def _():
        for x in range(3):
            tu[pl.ds(32 + x, 64, stride=40), :] = pltpu.roll(pe[0, x], shift, 1)

    for l in range(64):
        ru[l] = tu[pl.ds(40 * l + o0, 32), :]
        rv[l] = tv[pl.ds(40 * l + o0, 32), :]
        rp[l] = tp[pl.ds(40 * l + o0, 32), :]


def move_kernel(offsets, ru, rv, rp, east, north, corner, ou, ov, op, bu, bv, bp, ns, columns, sems):
    lanes = lane_index()
    o0, o1 = offsets[0, 0], offsets[0, 1]
    own_lane = lanes < 128 - o1
    own_row = lax.broadcasted_iota(jnp.int32, (8, 128), 0) < 8 - o0
    shift = lax.rem(128 - o1, 128)
    columns[8:392, :] = pltpu.roll(east[...], shift, 1)
    copies = []
    for b in range(8):
        ns[b, 0:32, :] = north[b]
        ns[b, 32:40, :] = corner[b]
        nrow = ns[b, pl.ds(o0, 32), :]
        for m in range(8):
            l = 8 * b + m
            for f, (src, buf) in enumerate(((ru, bu), (rv, bv), (rp, bp))):
                back = lax.rem(256 - (16 * m + 3 * f) - o1, 128)
                strip = pltpu.roll(nrow, back, 1)
                buf[l, 0:24, :] = jnp.where(own_lane, src[l, 0:24, :], strip[0:24])
                last = src[l, 24:32, :]
                if f > 0:
                    new = columns[pl.ds(192 * (f - 1) + 3 * l + o0, 8), :]
                    last = jnp.where(own_row, last, new)
                buf[l, 24:32, :] = jnp.where(own_lane, last, strip[24:32])
        for f, (buf, out) in enumerate(((bu, ou), (bv, ov), (bp, op))):
            part = pl.ds(8 * b, 8)
            copy = pltpu.make_async_copy(buf.at[part], out.at[part], sems.at[8 * f + b])
            copy.start()
            copies.append(copy)
    for copy in copies:
        copy.wait()


VMEM = pl.BlockSpec(memory_space=pltpu.VMEM)
SMEM = pl.BlockSpec(memory_space=pltpu.SMEM)
ANY = pl.BlockSpec(memory_space=pl.ANY)
HBM = pl.BlockSpec(memory_space=pltpu.HBM)


def sds(*shape):
    return jax.ShapeDtypeStruct(shape, F32)


def buffers(*shapes):
    return [pltpu.VMEM(shape, F32) for shape in shapes]


def call(body, out_shape, args, scratch=(), name=None, specs=None, outs=None, alias=None, us=0.05, vmem=16):
    specs = {} if specs is None else specs
    return pl.pallas_call(
        body,
        out_shape=out_shape,
        in_specs=[specs.get(k, VMEM) for k in range(len(args))],
        out_specs=jax.tree.map(lambda _: outs or VMEM, out_shape),
        scratch_shapes=list(scratch),
        input_output_aliases=alias or {},
        name=name,
        cost_estimate=pl.CostEstimate(flops=0, bytes_accessed=int(us * 3.2e6), transcendentals=0),
        compiler_params=pltpu.CompilerParams(vmem_limit_bytes=vmem << 20),
    )(*args)


def on_device(wind_east, wind_north, pressure, stiffness, parent_east, parent_north, parent_corner, offsets):
    nx, ny = lax.axis_size("gx"), lax.axis_size("gy")
    mat = jnp.asarray(band(), BF16)
    x_in, x_out = swaps(nx)
    y_in, y_out = swaps(ny)
    field, padded, outer = sds(64, 32, 128), sds(64, 48, 128), sds(64, 16, 128)
    dma = pltpu.SemaphoreType.DMA

    first, second = call(
        x_edges_kernel,
        (sds(576, 128), sds(576, 128)),
        (pressure, wind_east),
        buffers(*[(64, 8, 128)] * 4) + [dma((4,))],
        name="x_edges",
        specs={0: HBM, 1: HBM},
        vmem=53,
    )
    x2 = lax.ppermute(second, "gx", x_out)
    x1 = lax.ppermute(first, "gx", x_in)
    first, second = call(
        y_edges_kernel, (sds(6, 32, 128), sds(6, 32, 128)), (pressure, wind_north), name="y_edges"
    )
    y1 = lax.ppermute(first, "gy", y_in)
    y2 = lax.ppermute(second, "gy", y_out)
    inv, g = call(coefficients_kernel, (field, field), (stiffness,), name="coefficients")

    pe = parent_east.transpose(0, 2, 1, 3)
    pe_strip, pn_strip = call(
        parents_kernel,
        (sds(8, 8, 128), sds(8, 40, 128)),
        (pe, parent_north.transpose(0, 3, 2, 1), parent_corner.transpose(0, 2, 3, 1)),
        buffers((3 * 64 * 8, 128), (9, 40, 128)),
        name="parents",
    )

    u1, ex = call(
        functools.partial(across_kernel, True), (padded, outer), (pressure, wind_east), name="across1"
    )
    p1, v1, vh1, rest = call(
        functools.partial(inner_kernel, True),
        (field, field, field, outer),
        (pressure, wind_north, ex, inv, g, mat, y1, y2, pe_strip, pn_strip, pe),
        buffers((64, 16, 128)),
        name="inner1",
        specs={8: ANY, 9: ANY, 10: ANY},
        us=0.3,
    )
    p1, u1, first, second = call(
        functools.partial(outer_kernel, True),
        (field, padded, sds(384, 128), sds(384, 128)),
        (x1, x2, pressure, wind_east, inv, g, rest, p1, u1),
        buffers(*[(64, 16, 128)] * 5),
        name="outer1",
        alias={7: 0, 8: 1},
    )
    x2 = lax.ppermute(second, "gx", x_out)
    x1 = lax.ppermute(first, "gx", x_in)
    first, second = call(
        y_pack_kernel, (sds(4, 32, 128), sds(4, 32, 128)), (p1,), name="y_pack"
    )
    y1 = lax.ppermute(first, "gy", y_in)
    y2 = lax.ppermute(second, "gy", y_out)
    u2, ex = call(
        functools.partial(across_kernel, False), (padded, outer), (p1, u1), name="across2"
    )
    p2, v2, rest = call(
        functools.partial(inner_kernel, False),
        (field, field, outer),
        (p1, v1, ex, vh1, inv, g, mat, y1, y2),
        buffers((64, 16, 128)),
        name="inner2",
        us=0.3,
    )
    down_x = [(i, (i - 1) % nx) for i in range(nx)]
    down_y = [(j, (j - 1) % ny) for j in range(ny)]
    down = [(i * ny + j, (i - 1) % nx * ny + (j - 1) % ny) for i in range(nx) for j in range(ny)]
    p2, u2, east = call(
        functools.partial(outer_kernel, False),
        (field, padded, sds(384, 128)),
        (x1, x2, p1, u1, inv, g, rest, p2, u2, v2, pe),
        buffers(*[(64, 16, 128)] * 3),
        name="outer2",
        alias={7: 0, 8: 1},
    )
    east = lax.ppermute(east, "gx", down_x)
    corner = call(
        corner_pack_kernel, sds(8, 8, 128), (u2, v2, p2, pe_strip, pn_strip), name="corner_pack"
    )
    from_corner = lax.ppermute(corner, ("gx", "gy"), down)
    north = call(
        north_pack_kernel, sds(8, 32, 128), (u2, v2, p2, pn_strip, corner), name="north_pack"
    )
    north = lax.ppermute(north, "gy", down_y)
    offsets = jnp.pad(offsets.reshape(1, 2), ((0, 7), (0, 126)))
    ru, rv, rp = call(
        turn_kernel,
        (field, field, field),
        (offsets, u2, v2, p2, pe),
        buffers(*[(64 * 40, 128)] * 3),
        name="turn",
    )
    return call(
        move_kernel,
        (field, field, field),
        (offsets, ru, rv, rp, east, north, from_corner),
        buffers(*[(64, 32, 128)] * 3, (8, 40, 128), (392, 128))
        + [dma((24,))],
        name="move",
        outs=ANY,
    )


def solution(mesh):
    in_specs = (
        P(None, "gx", "gy"),
        P(None, "gx", "gy"),
        P(None, "gx", "gy"),
        P("gx", "gy"),
        P(None, None, None, "gy"),
        P(None, None, "gx", None),
        P(),
        P(),
    )
    out_specs = (P(None, "gx", "gy"), P(None, "gx", "gy"), P(None, "gx", "gy"))
    return jax.shard_map(
        on_device, mesh=mesh, in_specs=in_specs, out_specs=out_specs, check_vma=False
    )
```

```python
import functools

import jax
import jax.numpy as jnp
import numpy as np
from jax import lax
from jax.experimental import pallas as pl
from jax.experimental.pallas import tpu as pltpu
from jax.sharding import PartitionSpec as P

F32 = jnp.float32
BF16 = jnp.bfloat16

C1, C2, C3 = 0.45, 0.09, 0.01
CY = 0.01


def band():
    mat = np.zeros((256, 256), np.float32)
    for j in range(256):
        for k, w in ((1, 45.0), (2, -9.0), (3, 1.0)):
            mat[(j + k) % 256, j] = w
            mat[(j - k) % 256, j] = -w
    return mat


def swaps(count):
    inner = [(i, i ^ 1) for i in range(count)]
    outer = [(i, (i + 1) % count if i % 2 else (i - 1) % count) for i in range(count)]
    return inner, outer


def lane_index():
    return lax.broadcasted_iota(jnp.int32, (1, 128), 1)


def roll_lanes(value, shift):
    return pltpu.roll(value, shift % 128, 1)


def dy(ext, mat):
    hi = ext.astype(BF16)
    lo = (ext - hi.astype(F32)).astype(BF16)
    both = jnp.dot(jnp.concatenate([hi, lo], axis=0), mat, preferred_element_type=F32)
    return both[: ext.shape[0]] + both[ext.shape[0] :]


def pack_edges(rows, step, lanes):
    moved = [roll_lanes(row, m * step) for m, row in enumerate(rows)]
    low = high = moved[0]
    for m in range(1, len(moved)):
        low = jnp.where(lanes >= m * step, moved[m], low)
    for m in range(len(moved) - 1, 0, -1):
        high = jnp.where(lanes < m * step, moved[m], high)
    return low, high


def unpack_edges(north, south, m, step, lanes):
    mine = jnp.logical_and(lanes >= m * step, lanes < (m + 1) * step)
    return roll_lanes(jnp.where(mine, north, south), -m * step)


def write_edges(buffers, east, first, second):
    def write(ref, side):
        at = 0
        for buf, width in buffers[side]:
            a = 0 if side == 0 else 8 - width
            for l in range(64):
                ref[at + width * l : at + width * (l + 1), :] = buf[l, a : a + width, :]
            at += 64 * width

    @pl.when(east)
    def _():
        write(first, 1)
        write(second, 0)

    @pl.when(jnp.logical_not(east))
    def _():
        write(first, 0)
        write(second, 1)


def x_edges_kernel(p, u, first, second, pw, pe, uw, ue, sems):
    copies = []
    for k, (src, buf, at) in enumerate(((p, pw, 0), (u, uw, 0), (p, pe, 24), (u, ue, 24))):
        copies.append(pltpu.make_async_copy(src.at[:, at : at + 8, :], buf, sems.at[k]))
    for copy in copies:
        copy.start()
    for copy in copies:
        copy.wait()
    even = lax.axis_index("gx") % 2 == 0
    write_edges((((pw, 6), (uw, 3)), ((pe, 6), (ue, 3))), even, first, second)


def write_y_edges(field, count, step, at, first, second):
    lanes = lane_index()
    even = lax.axis_index("gy") % 2 == 0
    for b in range(64 // count):
        low, high = pack_edges([field[count * b + m] for m in range(count)], step, lanes)
        first[at + b] = jnp.where(even, high, low)
        second[at + b] = jnp.where(even, low, high)


def y_edges_kernel(p, v, first, second):
    write_y_edges(p, 16, 8, 0, first, second)
    write_y_edges(v, 32, 4, 4, first, second)


def y_pack_kernel(p, first, second):
    write_y_edges(p, 16, 8, 0, first, second)


def coefficients_kernel(s_ref, inv_ref, g_ref):
    s = s_ref[...]
    prev = None
    for l in range(64):
        if l == 0:
            div = 1.0 + s
        elif l < 63:
            div = 1.0 + 2.0 * s - s * prev
        else:
            div = 1.0 + s - s * prev
        inv = 1.0 / div
        inv_ref[l] = inv
        prev = s * inv
        g_ref[l] = prev


def difference(at):
    return C1 * (at(1) - at(-1)) - C2 * (at(2) - at(-2)) + C3 * (at(3) - at(-3))


def east_columns(out, field, pe, f):
    for l in range(64):
        out[3 * l : 3 * l + 3, :] = field[l, 0:3, :]

    @pl.when(lax.axis_index("gx") == 0)
    def _():
        for x in range(3):
            out[pl.ds(x, 64, stride=3), :] = pe[f, x]


def across_kernel(first_step, p, u, u_out, ex_out):
    du = 0 if first_step else 8
    for l in range(64):
        step = difference(lambda k: p[l, 5 + k : 29 + k, :])
        u_out[l, 13:37, :] = u[l, du + 5 : du + 29, :] - step
        ex_out[l] = difference(lambda k: u_out[l, 16 + k : 32 + k, :])


def inner_kernel(first_step, p, v, ex, *rest):
    if first_step:
        inv, g, mat, y2, y1, keep1, keep2, keep3, p_out, v_out, vh_out, rest_out, w_buf = rest
    else:
        vh_in, inv, g, mat, y2, y1, p_out, v_out, rest_out, w_buf = rest
    lanes = lane_index()
    gy = lax.axis_index("gy")
    even_y = gy % 2 == 0
    in_s = gy > 0
    in_n = gy < lax.axis_size("gy") - 1
    lane_ok = jnp.where(lanes < 64, jnp.where(in_n, 1.0, 0.0), jnp.where(in_s, 1.0, 0.0))

    def halos(at, levels, count, step):
        out = []
        for l in levels:
            a, c = y1[at + l // count], y2[at + l // count]
            north = jnp.where(in_n, jnp.where(even_y, a, c), 0.0)
            south = jnp.where(in_s, jnp.where(even_y, c, a), 0.0)
            out.append(unpack_edges(north, south, l % count, step, lanes))
        return jnp.concatenate(out, axis=0)

    w = jnp.zeros((16, 128), F32)
    for b in range(8):
        levels = range(8 * b, 8 * b + 8)
        halo = halos(0, levels, 16, 8)
        if first_step:
            vh = halos(4, levels, 32, 4)
        else:
            vh = vh_in[8 * b : 8 * b + 8].reshape(256, 128)
        own = p[8 * b : 8 * b + 8].reshape(256, 128)
        d = dy(jnp.concatenate([own, halo], axis=1), mat[...])
        v1 = v[8 * b : 8 * b + 8].reshape(256, 128) - CY * d[:, :128]
        vh = (vh - CY * d[:, 128:]) * lane_ok
        v_out[8 * b : 8 * b + 8] = v1.reshape(8, 32, 128)
        if first_step:
            vh_out[8 * b : 8 * b + 8] = vh.reshape(8, 32, 128)
        d2 = dy(jnp.concatenate([v1, vh], axis=1), mat[:, :128])
        left = own - CY * d2
        for m in range(8):
            l = 8 * b + m
            row = left[32 * m : 32 * m + 32]
            rest_out[l, 0:8, :] = row[0:8]
            rest_out[l, 8:16, :] = row[24:32]
            w = (row[8:24] - ex[l]) * inv[l, 8:24, :] + g[l, 8:24, :] * w
            w_buf[l] = w
    q = jnp.zeros((16, 128), F32)
    for l in range(63, -1, -1):
        q = w_buf[l] + g[l, 8:24, :] * q
        p_out[l, 8:24, :] = q


def outer_kernel(first_step, x1, x2, p, u, inv, g, rest, p_in, u_in, *tail):
    if first_step:
        p_out, u_out, first, second, pw, pe, uw, ue, w_buf = tail
    else:
        v, parent, p_out, u_out, east, pw, pe, w_buf = tail
    gx = lax.axis_index("gx")
    even = gx % 2 == 0
    in_w = gx > 0
    in_e = gx < lax.axis_size("gx") - 1

    def fill(ref, west):
        for l in range(64):
            part = jnp.where(in_w if west else in_e, ref[6 * l : 6 * l + 6, :], 0.0)
            if west:
                pw[l, 2:8, :] = part
            else:
                pe[l, 8:14, :] = part
            if first_step:
                part = ref[384 + 3 * l : 387 + 3 * l, :]
                if west:
                    uw[l, 5:8, :] = part
                else:
                    ue[l, 8:11, :] = part

    @pl.when(even)
    def _():
        fill(x1, False)
        fill(x2, True)

    @pl.when(jnp.logical_not(even))
    def _():
        fill(x1, True)
        fill(x2, False)

    rows = lax.broadcasted_iota(jnp.int32, (8, 128), 0)
    ok_w = jnp.where(rows < 3, jnp.where(in_w, 1.0, 0.0), 1.0)
    ok_e = jnp.where(rows >= 3, jnp.where(in_e, 1.0, 0.0), 1.0)
    w = jnp.zeros((16, 128), F32)
    for l in range(64):
        pw[l, 8:16, :] = p[l, 0:8, :]
        pe[l, 0:8, :] = p[l, 24:32, :]
        if first_step:
            uw[l, 8:16, :] = u[l, 0:8, :]
            ue[l, 0:8, :] = u[l, 24:32, :]
            old_w, old_e = uw[l, 5:13, :], ue[l, 5:13, :]
        else:
            old_w, old_e = u[l, 5:13, :], u[l, 37:45, :]
        u_out[l, 5:13, :] = (old_w - difference(lambda k: pw[l, 5 + k : 13 + k, :])) * ok_w
        u_out[l, 37:45, :] = (old_e - difference(lambda k: pe[l, 5 + k : 13 + k, :])) * ok_e
        rhs_w = rest[l, 0:8, :] - difference(lambda k: u_out[l, 8 + k : 16 + k, :])
        rhs_e = rest[l, 8:16, :] - difference(lambda k: u_out[l, 32 + k : 40 + k, :])
        rhs = jnp.concatenate([rhs_w, rhs_e], axis=0)
        il = jnp.concatenate([inv[l, 0:8, :], inv[l, 24:32, :]], axis=0)
        gl = jnp.concatenate([g[l, 0:8, :], g[l, 24:32, :]], axis=0)
        w = rhs * il + gl * w
        w_buf[l] = w
    q = jnp.zeros((16, 128), F32)
    for l in range(63, -1, -1):
        gl = jnp.concatenate([g[l, 0:8, :], g[l, 24:32, :]], axis=0)
        q = w_buf[l] + gl * q
        p_out[l, 0:8, :] = q[0:8]
        p_out[l, 24:32, :] = q[8:16]
        w_buf[l] = q
    if first_step:
        write_edges((((w_buf.at[:, 0:8, :], 6),), ((w_buf.at[:, 8:16, :], 6),)), even, first, second)
    else:
        east_columns(east.at[0:192], v, parent, 1)
        east_columns(east.at[192:384], w_buf, parent, 2)


def parents_kernel(pe, pn, pc, pe_strip, pn_strip, rows, cells):
    lanes = lane_index()
    for f in range(3):
        for x in range(3):
            rows[pl.ds(512 * f + x, 64, stride=8), :] = pe[f, x]
        for t in range(3):
            cells[3 * f + t, 0:32, 0:64] = pn[f, t]
            for x in range(3):
                cells[3 * f + t, 32 + x : 33 + x, 0:64] = pc[f, x, t : t + 1, :]
    lane = lax.broadcasted_iota(jnp.int32, (40, 128), 1)
    for b in range(8):
        strip = None
        for m in range(8):
            for f in range(3):
                at = 16 * m + 3 * f
                row = 512 * f + 8 * (8 * b + m)
                moved = roll_lanes(rows[row : row + 8, :], at)
                strip = moved if strip is None else jnp.where(lanes >= at, moved, strip)
        pe_strip[b] = strip
        strip = None
        for r in range(9):
            moved = jnp.take_along_axis(cells[r], 8 * b + lane // 16, axis=1, mode="promise_in_bounds")
            strip = moved if strip is None else jnp.where(lane % 16 >= r, moved, strip)
        pn_strip[b] = strip


def strip_of(fields, b, lanes):
    strip = None
    for m in range(8):
        for f, field in enumerate(fields):
            moved = roll_lanes(field(8 * b + m), 16 * m + 3 * f)
            strip = moved if strip is None else jnp.where(lanes >= 16 * m + 3 * f, moved, strip)
    return strip


def corner_pack_kernel(u, v, p, pe, pn, out):
    lanes = lane_index()
    west = lax.axis_index("gx") == 0
    south = lax.axis_index("gy") == 0
    fields = (lambda l: u[l, 8:16, :], lambda l: v[l, 0:8, :], lambda l: p[l, 0:8, :])
    for b in range(8):
        edge = jnp.where(west, pn[b, 32:40, :], pn[b, 0:8, :])
        strip = strip_of(fields, b, lanes)
        out[b] = jnp.where(south, edge, jnp.where(west, pe[b], strip))


def north_pack_kernel(u, v, p, pn, after, out):
    lanes = lane_index()
    south = lax.axis_index("gy") == 0
    fields = (lambda l: u[l, 8:40, :], lambda l: v[l], lambda l: p[l])
    for b in range(8):
        out[b] = jnp.where(south, pn[b, 0:32, :], strip_of(fields, b, lanes))


def turn_kernel(offsets, u, v, p, pe, ru, rv, rp, tu, tv, tp):
    o0 = offsets[0, 0]
    shift = lax.rem(128 - offsets[0, 1], 128)
    for l in range(64):
        tu[40 * l : 40 * l + 40, :] = pltpu.roll(u[l, 8:48, :], shift, 1)
        tv[40 * l : 40 * l + 32, :] = pltpu.roll(v[l], shift, 1)
        tp[40 * l : 40 * l + 32, :] = pltpu.roll(p[l], shift, 1)

    @pl.when(lax.axis_index("gx") == lax.axis_size("gx") - 1)
    def _():
        for x in range(3):
            tu[pl.ds(32 + x, 64, stride=40), :] = pltpu.roll(pe[0, x], shift, 1)

    for l in range(64):
        ru[l] = tu[pl.ds(40 * l + o0, 32), :]
        rv[l] = tv[pl.ds(40 * l + o0, 32), :]
        rp[l] = tp[pl.ds(40 * l + o0, 32), :]


def move_kernel(offsets, ru, rv, rp, east, north, corner, ou, ov, op, bu, bv, bp, ns, columns, sems):
    lanes = lane_index()
    o0, o1 = offsets[0, 0], offsets[0, 1]
    own_lane = lanes < 128 - o1
    own_row = lax.broadcasted_iota(jnp.int32, (8, 128), 0) < 8 - o0
    shift = lax.rem(128 - o1, 128)
    columns[8:392, :] = pltpu.roll(east[...], shift, 1)
    copies = []
    for b in range(8):
        ns[b, 0:32, :] = north[b]
        ns[b, 32:40, :] = corner[b]
        nrow = ns[b, pl.ds(o0, 32), :]
        for m in range(8):
            l = 8 * b + m
            for f, (src, buf) in enumerate(((ru, bu), (rv, bv), (rp, bp))):
                back = lax.rem(256 - (16 * m + 3 * f) - o1, 128)
                strip = pltpu.roll(nrow, back, 1)
                buf[l, 0:24, :] = jnp.where(own_lane, src[l, 0:24, :], strip[0:24])
                last = src[l, 24:32, :]
                if f > 0:
                    new = columns[pl.ds(192 * (f - 1) + 3 * l + o0, 8), :]
                    last = jnp.where(own_row, last, new)
                buf[l, 24:32, :] = jnp.where(own_lane, last, strip[24:32])
        for f, (buf, out) in enumerate(((bu, ou), (bv, ov), (bp, op))):
            part = pl.ds(8 * b, 8)
            copy = pltpu.make_async_copy(buf.at[part], out.at[part], sems.at[8 * f + b])
            copy.start()
            copies.append(copy)
    for copy in copies:
        copy.wait()


VMEM = pl.BlockSpec(memory_space=pltpu.VMEM)
SMEM = pl.BlockSpec(memory_space=pltpu.SMEM)
ANY = pl.BlockSpec(memory_space=pl.ANY)
HBM = pl.BlockSpec(memory_space=pltpu.HBM)


def sds(*shape):
    return jax.ShapeDtypeStruct(shape, F32)


def buffers(*shapes):
    return [pltpu.VMEM(shape, F32) for shape in shapes]


def call(body, out_shape, args, scratch=(), name=None, specs=None, outs=None, alias=None, us=0.05, vmem=16):
    specs = {} if specs is None else specs
    return pl.pallas_call(
        body,
        out_shape=out_shape,
        in_specs=[specs.get(k, VMEM) for k in range(len(args))],
        out_specs=jax.tree.map(lambda _: outs or VMEM, out_shape),
        scratch_shapes=list(scratch),
        input_output_aliases=alias or {},
        name=name,
        cost_estimate=pl.CostEstimate(flops=0, bytes_accessed=int(us * 3.2e6), transcendentals=0),
        compiler_params=pltpu.CompilerParams(vmem_limit_bytes=vmem << 20),
    )(*args)


def on_device(wind_east, wind_north, pressure, stiffness, parent_east, parent_north, parent_corner, offsets):
    nx, ny = lax.axis_size("gx"), lax.axis_size("gy")
    mat = jnp.asarray(band(), BF16)
    x_in, x_out = swaps(nx)
    y_in, y_out = swaps(ny)
    field, padded, outer = sds(64, 32, 128), sds(64, 48, 128), sds(64, 16, 128)
    dma = pltpu.SemaphoreType.DMA

    first, second = call(
        x_edges_kernel,
        (sds(576, 128), sds(576, 128)),
        (pressure, wind_east),
        buffers(*[(64, 8, 128)] * 4) + [dma((4,))],
        name="x_edges",
        specs={0: HBM, 1: HBM},
        vmem=53,
    )
    x2 = lax.ppermute(second, "gx", x_out)
    x1 = lax.ppermute(first, "gx", x_in)
    first, second = call(
        y_edges_kernel, (sds(6, 32, 128), sds(6, 32, 128)), (pressure, wind_north), name="y_edges"
    )
    y1 = lax.ppermute(first, "gy", y_in)
    y2 = lax.ppermute(second, "gy", y_out)
    inv, g = call(coefficients_kernel, (field, field), (stiffness,), name="coefficients")

    pe = parent_east.transpose(0, 2, 1, 3)
    pe_strip, pn_strip = call(
        parents_kernel,
        (sds(8, 8, 128), sds(8, 40, 128)),
        (pe, parent_north.transpose(0, 3, 2, 1), parent_corner.transpose(0, 2, 3, 1)),
        buffers((3 * 64 * 8, 128), (9, 40, 128)),
        name="parents",
    )

    u1, ex = call(
        functools.partial(across_kernel, True), (padded, outer), (pressure, wind_east), name="across1"
    )
    p1, v1, vh1, rest = call(
        functools.partial(inner_kernel, True),
        (field, field, field, outer),
        (pressure, wind_north, ex, inv, g, mat, y2, y1, pe_strip, pn_strip, pe),
        buffers((64, 16, 128)),
        name="inner1",
        specs={8: ANY, 9: ANY, 10: ANY},
        us=0.3,
    )
    p1, u1, first, second = call(
        functools.partial(outer_kernel, True),
        (field, padded, sds(384, 128), sds(384, 128)),
        (x1, x2, pressure, wind_east, inv, g, rest, p1, u1),
        buffers(*[(64, 16, 128)] * 5),
        name="outer1",
        alias={7: 0, 8: 1},
    )
    x2 = lax.ppermute(second, "gx", x_out)
    x1 = lax.ppermute(first, "gx", x_in)
    first, second = call(
        y_pack_kernel, (sds(4, 32, 128), sds(4, 32, 128)), (p1,), name="y_pack"
    )
    y1 = lax.ppermute(first, "gy", y_in)
    y2 = lax.ppermute(second, "gy", y_out)
    u2, ex = call(
        functools.partial(across_kernel, False), (padded, outer), (p1, u1), name="across2"
    )
    p2, v2, rest = call(
        functools.partial(inner_kernel, False),
        (field, field, outer),
        (p1, v1, ex, vh1, inv, g, mat, y2, y1),
        buffers((64, 16, 128)),
        name="inner2",
        us=0.3,
    )
    down_x = [(i, (i - 1) % nx) for i in range(nx)]
    down_y = [(j, (j - 1) % ny) for j in range(ny)]
    down = [(i * ny + j, (i - 1) % nx * ny + (j - 1) % ny) for i in range(nx) for j in range(ny)]
    p2, u2, east = call(
        functools.partial(outer_kernel, False),
        (field, padded, sds(384, 128)),
        (x1, x2, p1, u1, inv, g, rest, p2, u2, v2, pe),
        buffers(*[(64, 16, 128)] * 3),
        name="outer2",
        alias={7: 0, 8: 1},
    )
    east = lax.ppermute(east, "gx", down_x)
    corner = call(
        corner_pack_kernel, sds(8, 8, 128), (u2, v2, p2, pe_strip, pn_strip), name="corner_pack"
    )
    from_corner = lax.ppermute(corner, ("gx", "gy"), down)
    north = call(
        north_pack_kernel, sds(8, 32, 128), (u2, v2, p2, pn_strip, corner), name="north_pack"
    )
    north = lax.ppermute(north, "gy", down_y)
    offsets = jnp.pad(offsets.reshape(1, 2), ((0, 7), (0, 126)))
    ru, rv, rp = call(
        turn_kernel,
        (field, field, field),
        (offsets, u2, v2, p2, pe),
        buffers(*[(64 * 40, 128)] * 3),
        name="turn",
    )
    return call(
        move_kernel,
        (field, field, field),
        (offsets, ru, rv, rp, east, north, from_corner),
        buffers(*[(64, 32, 128)] * 3, (8, 40, 128), (392, 128))
        + [dma((24,))],
        name="move",
        outs=ANY,
    )


def solution(mesh):
    in_specs = (
        P(None, "gx", "gy"),
        P(None, "gx", "gy"),
        P(None, "gx", "gy"),
        P("gx", "gy"),
        P(None, None, None, "gy"),
        P(None, None, "gx", None),
        P(),
        P(),
    )
    out_specs = (P(None, "gx", "gy"), P(None, "gx", "gy"), P(None, "gx", "gy"))
    return jax.shard_map(
        on_device, mesh=mesh, in_specs=in_specs, out_specs=out_specs, check_vma=False
    )
```
